32 devices in a mesh: section: 4 (over z), expert: 8 (over y, x, core).
Axes of the slice: x: 2, y: 2, z: 4, core: 2. Of those that a mesh axis runs over, the one named last changes fastest.
Arguments:
- features: bfloat16 [2, 512, 2048], P(None, 'expert'), may hold values from -6 to 6
- labels: int32 [2, 512], P(None, 'expert'), may hold values 0 or 1
- routes: int32 [4, 2, 512, 1], P('section', None, 'expert'), may hold values from 0 to 7; in each aligned block of 64 rows (0 to 63, 64 to 127, ..., all dimensions but the last counted through in order) at most 12 rows name the same one
- route_gates: float32 [4, 2, 512], P('section', None, 'expert'), may hold values from 0.25 to 1
- gate_weight: bfloat16 [4, 8, 2048, 256], P('section', 'expert'), may hold values from -0.125 to 0.125
- up_weight: bfloat16 [4, 8, 2048, 256], P('section', 'expert'), may hold values from -0.125 to 0.125
- down_weight: bfloat16 [4, 8, 256, 2048], P('section', 'expert'), may hold values from -0.375 to 0.375
- lowrank_in: bfloat16 [4, 2048, 128], P('section'), may hold values from -0.125 to 0.125
- lowrank_out: bfloat16 [4, 128, 2048], P('section'), may hold values from -0.5 to 0.5
- head_weight: float32 [2048], replicated, may hold values from -0.5 to 0.5
Outputs:
- grad_gate: float32 [4, 8, 2048, 256], P('section', 'expert')
- grad_up: float32 [4, 8, 2048, 256], P('section', 'expert')
- grad_down: float32 [4, 8, 256, 2048], P('section', 'expert')
- grad_lowrank_in: float32 [4, 2048, 128], P('section', 'expert')
- grad_lowrank_out: float32 [4, 128, 2048], P('section', None, 'expert')
The draws below stay inside these ranges and needn't reach their ends.
Inputs may be any that keep to these rules, and one draw needn't show every extreme that they name: `routes`: in each layer and micro-batch the 64 rows of one device name one expert at most 12 times, and 12 is reached in every draw.
All inputs are finite; a program needn't handle non-finite values. No bound on the sum of `labels` on one device may be relied on, other than what follows from the above.
Results may differ from the reference program's by a relative error of at most 0.04.
Values may be sent and summed in bfloat16 or wider, within the bound.
A program may use at most 128 MiB of HBM per device.

```python
import math
import jax
import jax.numpy as jnp
import numpy as np
from jax import lax

D = 2048
FE = 256
RANK = 128
MB = 2
ROWS = 64
EXPERTS = 8
ROWS_ALL = 512
CAP = 12
N_SECTION = 4
N_EXPERT = 8


def with_ends(result, rng, low, high):
    index_at = [jax.random.randint(jax.random.fold_in(rng, axis), (), 0, length) for axis, length in enumerate(result.shape)]
    longest = result.shape.index(max(result.shape))
    next_to = index_at[:longest] + [(index_at[longest] + 1) % result.shape[longest]] + index_at[longest + 1:]
    return result.at[tuple(index_at)].set(low).at[tuple(next_to)].set(high)


def steps_of(key, dims, pieces, low, top_value):
    loudness, own = 1.0, jax.random.fold_in(key, 6)
    for position, blocks in pieces:
        heights = jnp.exp(jax.random.uniform(jax.random.fold_in(own, position), (blocks,), jnp.float32, low / len(pieces), top_value / len(pieces)))
        loudness = loudness * jnp.repeat(heights, dims[position] // blocks).reshape([-1 if axis == position else 1 for axis in range(len(dims))])
    return loudness


def deal_out(own_key, own, number, rows, amount, top, limit, slope):
    order = jax.random.permutation(own_key, amount)
    heavy_load, usual = portions_of(amount, rows * top, limit, slope, True), portions_of(amount, rows * top, limit, slope, False)
    places = jnp.arange(amount)

    def named(sizes, offset_by):
        used = int((sizes > 0).sum())
        fixed = max(1, used // 4)
        shifted = fixed + (places - fixed + offset_by * (used - fixed)) % max(1, amount - fixed)
        return jnp.zeros((amount,), jnp.int32).at[order[jnp.where(places < fixed, places, shifted)]].set(jnp.asarray(sizes, jnp.int32))

    sizes = jnp.where(number % 4 == 0, named(heavy_load, number // 4), named(usual, number - number // 4 - 1))
    mixed = jax.random.permutation(jax.random.fold_in(own, 3), amount)
    giver, taker = mixed[0:amount // 2 * 2:2], mixed[1:amount // 2 * 2:2]
    room = jnp.minimum(sizes[giver] - 1, limit - sizes[taker]) // 2
    room = jnp.where((giver == order[0]) | (taker == order[0]) | (sizes[taker] == 0), 0, jnp.maximum(room, 0))
    shifted = jax.random.randint(jax.random.fold_in(own, 4), (amount // 2,), 0, 1 << 20) % (room + 1)
    sizes = sizes.at[giver].add(-shifted).at[taker].add(shifted)
    items = jnp.searchsorted(jnp.cumsum(sizes), jnp.arange(rows * top), side="right").astype(jnp.int32)
    table = items.reshape(top, rows).T
    table = table[jax.random.permutation(jax.random.fold_in(own, 1), rows)]
    offset_by = jax.random.randint(jax.random.fold_in(own, 2), (rows, 1), 0, top)
    return jnp.take_along_axis(table, (jnp.arange(top)[None, :] + offset_by) % top, axis=1)


def portions_of(number_of, total, reach, lean, full):
    loads = [(1 << 20) // math.isqrt(standing ** lean) + 1 for standing in range(1, number_of + 1)]
    largest = reach if full else min(reach, max(-(-total // number_of), total * loads[0] // sum(loads)))
    least = 1 if total - largest >= number_of - 1 else 0
    holding, spare = [largest] + [least] * (number_of - 1), total - largest - least * (number_of - 1)
    while spare > 0:
        candidates = [i for i in range(1, number_of) if holding[i] < largest] or [i for i in range(1, number_of) if holding[i] < reach]
        whole, left = sum([loads[i] for i in candidates]), spare
        for i in candidates:
            more = min(reach - holding[i], max(1, left * loads[i] // whole), spare)
            holding[i] = holding[i] + more
            spare = spare - more
    return np.array(holding)


def scatter_about(key, extent, deviation, reach, split=(), held_as=jnp.bfloat16):
    result = deviation * jax.random.normal(key, extent, jnp.float32)
    if split:
        result = result * steps_of(key, extent, split, -0.22, 0.18)
    return jnp.clip(result, -reach, reach).astype(held_as)


def setup_inputs(seed: int = 0) -> dict:
    key_of = jax.random.split(jax.random.key(seed), 11)
    features = scatter_about(key_of[0], (MB, ROWS_ALL, D), 1.0, 6.0, ((1, 8),))
    labels = with_ends((jax.random.randint(key_of[1], (MB, ROWS_ALL), 0, 3) < 1).astype(jnp.int32), jax.random.fold_in(key_of[1], 1), 0, 1)
    routes_keys = jax.random.split(jax.random.fold_in(key_of[2], 1), N_SECTION * MB * ROWS_ALL // ROWS)
    routes_turns = jax.random.permutation(jax.random.fold_in(key_of[2], 3), N_SECTION * MB * ROWS_ALL // ROWS)
    routes = jax.vmap(lambda own, number: deal_out(jax.random.fold_in(key_of[2], 2), own, number, ROWS, EXPERTS, 1, CAP, 2))(routes_keys, routes_turns).reshape((N_SECTION, MB, ROWS_ALL, 1))
    route_gates = jnp.clip(0.25 + 0.75 * jax.random.uniform(key_of[3], (N_SECTION, MB, ROWS_ALL), jnp.float32) ** steps_of(key_of[3], (N_SECTION, MB, ROWS_ALL), ((0, 4), (2, 8)), -0.2, 0.2), 0.25, 1.0)
    gate_weight = scatter_about(key_of[4], (N_SECTION, EXPERTS, D, FE), D ** -0.5, 0.125, ((0, 4), (1, 8)))
    up_weight = scatter_about(key_of[5], (N_SECTION, EXPERTS, D, FE), D ** -0.5, 0.125, ((0, 4), (1, 8)))
    down_weight = scatter_about(key_of[6], (N_SECTION, EXPERTS, FE, D), FE ** -0.5, 0.375, ((0, 4), (1, 8)))
    lowrank_in = scatter_about(key_of[7], (N_SECTION, D, RANK), D ** -0.5, 0.125, ((0, 4),))
    lowrank_out = scatter_about(key_of[8], (N_SECTION, RANK, D), RANK ** -0.5, 0.5, ((0, 4),))
    head_weight = scatter_about(key_of[9], (D,), (D // 16) ** -0.5, 0.5, (), jnp.float32)
    return {"features": features, "labels": labels, "routes": routes, "route_gates": route_gates, "gate_weight": gate_weight, "up_weight": up_weight, "down_weight": down_weight, "lowrank_in": lowrank_in, "lowrank_out": lowrank_out, "head_weight": head_weight}


epsilon = 1e-06

def rms_scale(values):
    widened = values.astype(jnp.float32)
    return lax.rsqrt(lax.optimization_barrier(jnp.mean(widened * widened, axis=-1, keepdims=True)) + epsilon)

def norm_back(values, row_scale, grad_norm):
    widened = values.astype(jnp.float32)
    inner_mean = lax.optimization_barrier(jnp.mean(grad_norm * widened, axis=-1, keepdims=True))
    return row_scale * grad_norm - widened * (row_scale * row_scale * row_scale) * inner_mean

def expert_forward(slot_rows, gate_mat, up_mat, down_mat):
    gate_pre = jnp.dot(slot_rows, gate_mat, preferred_element_type=jnp.float32)
    up_pre = jnp.dot(slot_rows, up_mat, preferred_element_type=jnp.float32)
    hidden = (gate_pre * jax.nn.sigmoid(gate_pre) * up_pre).astype(jnp.bfloat16)
    return jnp.dot(hidden, down_mat, preferred_element_type=jnp.float32).astype(jnp.bfloat16)

def expert_backward(slot_rows, grad_out, gate_mat, up_mat, down_mat):
    gate_pre = jnp.dot(slot_rows, gate_mat, preferred_element_type=jnp.float32)
    up_pre = jnp.dot(slot_rows, up_mat, preferred_element_type=jnp.float32)
    gate_sig = jax.nn.sigmoid(gate_pre)
    gate_act = gate_pre * gate_sig
    hidden = (gate_act * up_pre).astype(jnp.bfloat16)
    grad_hidden = jnp.dot(grad_out, down_mat.T, preferred_element_type=jnp.float32)
    grad_gate = (grad_hidden * up_pre * (gate_sig * (1.0 + gate_pre * (1.0 - gate_sig)))).astype(jnp.bfloat16)
    grad_up = (grad_hidden * gate_act).astype(jnp.bfloat16)
    grad_slots = (jnp.dot(grad_gate, gate_mat.T, preferred_element_type=jnp.float32) + jnp.dot(grad_up, up_mat.T, preferred_element_type=jnp.float32)).astype(jnp.bfloat16)
    part_gate = jnp.dot(slot_rows.T, grad_gate, preferred_element_type=jnp.float32)
    part_up = jnp.dot(slot_rows.T, grad_up, preferred_element_type=jnp.float32)
    part_down = jnp.dot(hidden.T, grad_out, preferred_element_type=jnp.float32)
    return (grad_slots, part_gate, part_up, part_down)

def lowrank_parts(values, matrix_in):
    row_scale = rms_scale(values)
    normed = (values.astype(jnp.float32) * row_scale).astype(jnp.bfloat16)
    inner_pre = jnp.dot(normed, matrix_in, preferred_element_type=jnp.float32)
    inner_sig = jax.nn.sigmoid(inner_pre)
    inner_act = (inner_pre * inner_sig).astype(jnp.bfloat16)
    return (row_scale, normed, inner_pre, inner_sig, inner_act)

def lowrank_forward(values, matrix_in, matrix_out):
    row_scale, normed, inner_pre, inner_sig, inner_act = lowrank_parts(values, matrix_in)
    return (values.astype(jnp.float32) + jnp.dot(inner_act, matrix_out, preferred_element_type=jnp.float32)).astype(jnp.bfloat16)

def lowrank_backward(values, grad_rows, matrix_in, matrix_out):
    row_scale, normed, inner_pre, inner_sig, inner_act = lowrank_parts(values, matrix_in)
    grad_act = jnp.dot(grad_rows, matrix_out.T, preferred_element_type=jnp.float32)
    grad_pre = (grad_act * (inner_sig * (1.0 + inner_pre * (1.0 - inner_sig)))).astype(jnp.bfloat16)
    grad_norm = jnp.dot(grad_pre, matrix_in.T, preferred_element_type=jnp.float32)
    grad_input = (grad_rows.astype(jnp.float32) + norm_back(values, row_scale, grad_norm)).astype(jnp.bfloat16)
    part_in = jnp.dot(normed.T, grad_pre, preferred_element_type=jnp.float32)
    part_out = jnp.dot(inner_act.T, grad_rows, preferred_element_type=jnp.float32)
    return (grad_input, part_in, part_out)

def head_grad(values, targets, head_weight):
    row_scale = rms_scale(values)
    logits = row_scale[:, 0] * lax.optimization_barrier(jnp.sum(values.astype(jnp.float32) * head_weight[None, :], axis=1))
    grad_logit = jax.nn.sigmoid(logits) - targets.astype(jnp.float32)
    return norm_back(values, row_scale, grad_logit[:, None] * head_weight[None, :]).astype(jnp.bfloat16)

def slot_positions(expert_ids):
    chosen = (expert_ids[:, None] == jnp.arange(N_EXPERT, dtype=jnp.int32)[None, :]).astype(jnp.int32)
    ranking = jnp.cumsum(chosen, axis=0) - 1
    return lax.optimization_barrier(jnp.sum(chosen * ranking, axis=1)).astype(jnp.int32)

def moe_forward(values, expert_ids, gate_row, gate_mats, up_mats, down_mats, slot_limit):
    row_scale = rms_scale(values)
    normed = (values.astype(jnp.float32) * row_scale).astype(jnp.bfloat16)
    slot_index = slot_positions(expert_ids)
    buffer = jnp.zeros((N_EXPERT, slot_limit, values.shape[1]), jnp.bfloat16).at[expert_ids, slot_index].set(normed)
    served = lax.map(lambda packed: expert_forward(packed[0], packed[1], packed[2], packed[3]), (buffer, gate_mats, up_mats, down_mats))
    layer_out = values.astype(jnp.float32) + gate_row[:, None] * served[expert_ids, slot_index].astype(jnp.float32)
    return layer_out.astype(jnp.bfloat16)

def moe_backward(values, grad_rows, expert_ids, gate_row, gate_mats, up_mats, down_mats, slot_limit):
    row_scale = rms_scale(values)
    normed = (values.astype(jnp.float32) * row_scale).astype(jnp.bfloat16)
    slot_index = slot_positions(expert_ids)
    grad_out = (gate_row[:, None] * grad_rows.astype(jnp.float32)).astype(jnp.bfloat16)
    empty = jnp.zeros((N_EXPERT, slot_limit, values.shape[1]), jnp.bfloat16)
    slot_rows = empty.at[expert_ids, slot_index].set(normed)
    slot_grads = empty.at[expert_ids, slot_index].set(grad_out)
    grad_slots, part_gate, part_up, part_down = lax.map(lambda packed: expert_backward(packed[0], packed[1], packed[2], packed[3], packed[4]), (slot_rows, slot_grads, gate_mats, up_mats, down_mats))
    grad_norm = grad_slots[expert_ids, slot_index].astype(jnp.float32)
    grad_input = (grad_rows.astype(jnp.float32) + norm_back(values, row_scale, grad_norm)).astype(jnp.bfloat16)
    return (grad_input, part_gate, part_up, part_down)

def reference(features, labels, routes, route_gates, gate_weight, up_weight, down_weight, lowrank_in, lowrank_out, head_weight):
    feature_width = features.shape[-1]
    slot_limit = MB * N_EXPERT * CAP
    hidden_rows = features.reshape(-1, feature_width)
    moe_inputs = []
    for layer_id in range(N_SECTION):
        moe_inputs.append(hidden_rows)
        hidden_rows = moe_forward(hidden_rows, routes[layer_id].reshape(-1), route_gates[layer_id].reshape(-1), gate_weight[layer_id], up_weight[layer_id], down_weight[layer_id], slot_limit)
    low_inputs = [None] * N_SECTION
    for layer_id in reversed(range(N_SECTION)):
        low_inputs[layer_id] = hidden_rows
        hidden_rows = lowrank_forward(hidden_rows, lowrank_in[layer_id], lowrank_out[layer_id])
    grad_rows = head_grad(hidden_rows, labels.reshape(-1), head_weight)
    grads_in = [None] * N_SECTION
    grads_out = [None] * N_SECTION
    for layer_id in range(N_SECTION):
        grad_rows, part_in, part_out = lowrank_backward(low_inputs[layer_id], grad_rows, lowrank_in[layer_id], lowrank_out[layer_id])
        grads_in[layer_id] = part_in
        grads_out[layer_id] = part_out
    grads_gate = [None] * N_SECTION
    grads_up = [None] * N_SECTION
    grads_down = [None] * N_SECTION
    for layer_id in reversed(range(N_SECTION)):
        grad_rows, part_gate, part_up, part_down = moe_backward(moe_inputs[layer_id], grad_rows, routes[layer_id].reshape(-1), route_gates[layer_id].reshape(-1), gate_weight[layer_id], up_weight[layer_id], down_weight[layer_id], slot_limit)
        grads_gate[layer_id] = part_gate
        grads_up[layer_id] = part_up
        grads_down[layer_id] = part_down
    return (jnp.stack(grads_gate), jnp.stack(grads_up), jnp.stack(grads_down), jnp.stack(grads_in), jnp.stack(grads_out))
```

```python
import jax
import jax.numpy as jnp
from jax import lax
from jax.sharding import PartitionSpec as P

epsilon = 1e-06


def shifted(value, axis, steps):
    count = lax.axis_size(axis)
    first, last = (max(0, -steps), min(count, count - steps))
    return lax.ppermute(value, axis, [(source, source + steps) for source in range(first, last)])


def rms_scale(values):
    widened = values.astype(jnp.float32)
    return lax.rsqrt(jnp.mean(widened * widened, axis=-1, keepdims=True) + epsilon)


def norm_back(values, row_scale, grad_norm):
    widened = values.astype(jnp.float32)
    inner_mean = jnp.mean(grad_norm * widened, axis=-1, keepdims=True)
    return row_scale * grad_norm - widened * (row_scale * row_scale * row_scale) * inner_mean


def lowrank_parts(values, matrix_in):
    row_scale = rms_scale(values)
    normed = (values.astype(jnp.float32) * row_scale).astype(jnp.bfloat16)
    inner_pre = jnp.dot(normed, matrix_in, preferred_element_type=jnp.float32)
    inner_sig = jax.nn.sigmoid(inner_pre)
    inner_act = (inner_pre * inner_sig).astype(jnp.bfloat16)
    return (row_scale, normed, inner_pre, inner_sig, inner_act)


def head_grad(values, targets, head_weight):
    row_scale = rms_scale(values)
    logits = row_scale[:, 0] * jnp.sum(values.astype(jnp.float32) * head_weight[None, :], axis=1)
    grad_logit = jax.nn.sigmoid(logits) - targets.astype(jnp.float32)
    return norm_back(values, row_scale, grad_logit[:, None] * head_weight[None, :]).astype(
        jnp.bfloat16
    )


def route_table(expert_ids, expert_count, capacity):
    chosen = (expert_ids[:, None] == jnp.arange(expert_count, dtype=jnp.int32)[None, :]).astype(
        jnp.int32
    )
    ranking = jnp.cumsum(chosen, axis=0) - 1
    slot_index = jnp.sum(chosen * ranking, axis=1)
    target_slot = expert_ids * capacity + slot_index
    slot_grid = jnp.arange(expert_count * capacity, dtype=jnp.int32)
    return (slot_grid[:, None] == target_slot[None, :]).astype(jnp.bfloat16)


def local(
    features,
    labels,
    routes,
    route_gates,
    gate_weight,
    up_weight,
    down_weight,
    lowrank_in,
    lowrank_out,
    head_weight,
):
    section_count = lax.axis_size("section")
    section_index = lax.axis_index("section")
    expert_count = lax.axis_size("expert")
    micro_count, row_count, width = features.shape
    capacity = micro_count * min(row_count, max(2, 3 * row_count // (2 * expert_count)))
    last = section_count - 1
    gate_mat = gate_weight[0, 0]
    up_mat = up_weight[0, 0]
    down_mat = down_weight[0, 0]
    table = route_table(routes.reshape(-1), expert_count, capacity)
    gates = route_gates.reshape(-1)[:, None]
    all_in = lax.all_gather(lowrank_in[0], "section")
    all_out = lax.all_gather(lowrank_out[0], "section")

    def exchange(rows):
        return lax.all_to_all(rows, "expert", split_axis=0, concat_axis=0, tiled=True)

    def spread(rows):
        placed = jnp.dot(table, rows, preferred_element_type=jnp.float32).astype(jnp.bfloat16)
        return exchange(placed.reshape(expert_count, capacity, width)).reshape(-1, width)

    def collect(rows):
        back = exchange(rows.reshape(expert_count, capacity, width)).reshape(-1, width)
        return lax.dot_general(
            table, back, (((0,), (0,)), ((), ())), preferred_element_type=jnp.float32
        )

    def keep(kept, value, tick):
        return jnp.where(section_index == tick, value, kept)

    rows = features.reshape(-1, width)
    kept_rows = rows
    kept_slots = jnp.zeros((expert_count * capacity, width), jnp.bfloat16)
    for tick in range(section_count):
        normed = (rows.astype(jnp.float32) * rms_scale(rows)).astype(jnp.bfloat16)
        slots = spread(normed)
        kept_rows = keep(kept_rows, rows, tick)
        kept_slots = keep(kept_slots, slots, tick)
        gate_pre = jnp.dot(slots, gate_mat, preferred_element_type=jnp.float32)
        up_pre = jnp.dot(slots, up_mat, preferred_element_type=jnp.float32)
        hidden = (gate_pre * jax.nn.sigmoid(gate_pre) * up_pre).astype(jnp.bfloat16)
        served = jnp.dot(hidden, down_mat, preferred_element_type=jnp.float32).astype(jnp.bfloat16)
        rows = (rows.astype(jnp.float32) + gates * collect(served)).astype(jnp.bfloat16)
        if tick < last:
            rows = shifted(rows, "section", 1)

    low_inputs = [None] * section_count
    for layer in reversed(range(section_count)):
        low_inputs[layer] = rows
        inner_act = lowrank_parts(rows, all_in[layer])[4]
        rows = (
            rows.astype(jnp.float32)
            + jnp.dot(inner_act, all_out[layer], preferred_element_type=jnp.float32)
        ).astype(jnp.bfloat16)
    grads = head_grad(rows, labels.reshape(-1), head_weight)
    parts_in, parts_out = [], []
    for layer in range(section_count):
        values = low_inputs[layer]
        row_scale, normed, inner_pre, inner_sig, inner_act = lowrank_parts(values, all_in[layer])
        grad_act = jnp.dot(grads, all_out[layer].T, preferred_element_type=jnp.float32)
        grad_pre = (grad_act * (inner_sig * (1.0 + inner_pre * (1.0 - inner_sig)))).astype(
            jnp.bfloat16
        )
        grad_norm = jnp.dot(grad_pre, all_in[layer].T, preferred_element_type=jnp.float32)
        parts_in.append(jnp.dot(normed.T, grad_pre, preferred_element_type=jnp.float32))
        parts_out.append(jnp.dot(grads.T, inner_act, preferred_element_type=jnp.float32))
        grads = (grads.astype(jnp.float32) + norm_back(values, row_scale, grad_norm)).astype(
            jnp.bfloat16
        )

    def share(parts):
        stacked = jnp.stack(parts).astype(jnp.bfloat16)
        stacked = jnp.where(section_index == last, stacked, jnp.zeros_like(stacked))
        stacked = stacked.reshape(section_count * width, -1)
        return lax.psum_scatter(
            stacked, ("section", "expert"), scatter_dimension=0, tiled=True
        ).astype(jnp.float32)

    share_in = share(parts_in)
    share_out = share(parts_out).T

    gate_pre = jnp.dot(kept_slots, gate_mat, preferred_element_type=jnp.float32)
    up_pre = jnp.dot(kept_slots, up_mat, preferred_element_type=jnp.float32)
    gate_sig = jax.nn.sigmoid(gate_pre)
    gate_act = gate_pre * gate_sig
    hidden = (gate_act * up_pre).astype(jnp.bfloat16)
    gate_slope = up_pre * (gate_sig * (1.0 + gate_pre * (1.0 - gate_sig)))
    kept_scale = rms_scale(kept_rows)
    kept_out = jnp.zeros_like(kept_slots)
    for tick in reversed(range(section_count)):
        slots = spread((gates * grads.astype(jnp.float32)).astype(jnp.bfloat16))
        kept_out = keep(kept_out, slots, tick)
        if tick == 0:
            break
        grad_hidden = lax.dot_general(
            slots, down_mat, (((1,), (1,)), ((), ())), preferred_element_type=jnp.float32
        )
        grad_gate = (grad_hidden * gate_slope).astype(jnp.bfloat16)
        grad_up = (grad_hidden * gate_act).astype(jnp.bfloat16)
        grad_slots = (
            jnp.dot(grad_gate, gate_mat.T, preferred_element_type=jnp.float32)
            + jnp.dot(grad_up, up_mat.T, preferred_element_type=jnp.float32)
        ).astype(jnp.bfloat16)
        grad_norm = collect(grad_slots)
        grads = (
            grads.astype(jnp.float32) + norm_back(kept_rows, kept_scale, grad_norm)
        ).astype(jnp.bfloat16)
        grads = shifted(grads, "section", -1)
    grad_hidden = lax.dot_general(
        kept_out, down_mat, (((1,), (1,)), ((), ())), preferred_element_type=jnp.float32
    )
    grad_gate = (grad_hidden * gate_slope).astype(jnp.bfloat16)
    grad_up = (grad_hidden * gate_act).astype(jnp.bfloat16)
    sum_gate = jnp.dot(kept_slots.T, grad_gate, preferred_element_type=jnp.float32)
    sum_up = jnp.dot(kept_slots.T, grad_up, preferred_element_type=jnp.float32)
    sum_down = jnp.dot(hidden.T, kept_out, preferred_element_type=jnp.float32)
    return (
        sum_gate[None, None],
        sum_up[None, None],
        sum_down[None, None],
        share_in[None],
        share_out[None],
    )


def solution(mesh):
    return jax.shard_map(
        local,
        mesh=mesh,
        in_specs=(
            P(None, "expert", None),
            P(None, "expert"),
            P("section", None, "expert", None),
            P("section", None, "expert"),
            P("section", "expert", None, None),
            P("section", "expert", None, None),
            P("section", "expert", None, None),
            P("section", None, None),
            P("section", None, None),
            P(),
        ),
        out_specs=(
            P("section", "expert", None, None),
            P("section", "expert", None, None),
            P("section", "expert", None, None),
            P("section", "expert", None),
            P("section", None, "expert"),
        ),
        check_vma=False,
    )
```

```python
import functools

import jax
import jax.numpy as jnp
from jax import lax
from jax.experimental import pallas as pl
from jax.experimental.pallas import tpu as pltpu
from jax.sharding import PartitionSpec as P

epsilon = 1e-06
MESH = pl.DeviceIdType.MESH
f32, bf16 = jnp.float32, jnp.bfloat16
TILE = 16
NN = (((1,), (0,)), ((), ()))
NT = (((1,), (1,)), ((), ()))
TN = (((0,), (0,)), ((), ()))


def mm(left, right, dims=NN):
    return lax.dot_general(left, right, dims, preferred_element_type=f32)


def rms_scale(widened):
    return lax.rsqrt(jnp.mean(widened * widened, axis=-1, keepdims=True) + epsilon)


def norm_back(widened, row_scale, grad_norm):
    inner_mean = jnp.mean(grad_norm * widened, axis=-1, keepdims=True)
    return row_scale * grad_norm - widened * (row_scale * row_scale * row_scale) * inner_mean


def sigmoid(values):
    return jax.nn.sigmoid(values)


def kernel(
    sections, experts, slot,
    feat, label, id_row, id_col, gates, gate_w, up_w, down_w, low, head,
    out_gate, out_up, out_down, out_low,
    h_in, h_out, g_in, scale, spread, gather, outgoing, slots, back, slot_grads,
    gate_act, gate_slope, hidden, grad_gate, grad_up,
    low_all, low_rows, low_grads, low_scale, low_act, low_slope, low_pre, parts, shares, share_in,
    stage, out_sem,
    x_send, x_recv, hop_send, hop_recv, lw_send, lw_recv, lb_send, lb_recv,
    p_send, p_recv, q_send, q_recv,
):
    micro, rows, width = feat.shape
    count = experts * slot
    piece = width // experts
    last = sections - 1
    sec, me = lax.axis_index("section"), lax.axis_index("expert")
    mine = pl.ds(pl.multiple_of(me * piece, piece), piece)

    barrier = pltpu.get_barrier_semaphore()

    @pl.loop(1, experts)
    def _(k):
        pl.semaphore_signal(
            barrier, inc=1, device_id=(sec, lax.rem(me + k, experts)), device_id_type=MESH
        )

    @pl.loop(1, sections)
    def _(k):
        pl.semaphore_signal(
            barrier, inc=1, device_id=(lax.rem(sec + k, sections), me), device_id_type=MESH
        )

    pl.semaphore_wait(barrier, experts + sections - 2)

    def low_copy(source):
        return pltpu.make_async_remote_copy(
            src_ref=low.at[:, mine, :], dst_ref=low_all.at[source, :, mine, :],
            send_sem=lw_send, recv_sem=lw_recv.at[source],
            device_id=(last, me), device_id_type=MESH,
        )

    def low_spread(peer, owner):
        part = pl.ds(pl.multiple_of(owner * piece, piece), piece)
        view = low_all.at[pl.ds(0, last), :, part, :]
        return pltpu.make_async_remote_copy(
            src_ref=view, dst_ref=view, send_sem=lb_send.at[peer], recv_sem=lb_recv.at[owner],
            device_id=(sec, peer), device_id_type=MESH,
        )

    def exchange(phase, m, peer, owner, target):
        return pltpu.make_async_remote_copy(
            src_ref=outgoing.at[m, peer], dst_ref=target.at[m, owner],
            send_sem=x_send.at[phase, m, peer], recv_sem=x_recv.at[phase, m, owner],
            device_id=(sec, peer), device_id_type=MESH,
        )

    def send_slots(phase, m, target):
        @pl.loop(1, experts)
        def _(k):
            exchange(phase, m, lax.rem(me + k, experts), me, target).start()

        target[m, me] = outgoing[m, me]

    def wait_slots(phase, m, target):
        @pl.loop(1, experts)
        def _(k):
            peer = lax.rem(me + k, experts)
            exchange(phase, m, peer, peer, target).wait_recv()

    def wait_sent(phase, m, target):
        @pl.loop(1, experts)
        def _(k):
            exchange(phase, m, lax.rem(me + k, experts), me, target).wait_send()

    def hop(way, m, source, target, to):
        return pltpu.make_async_remote_copy(
            src_ref=source.at[m], dst_ref=target.at[m],
            send_sem=hop_send.at[way, m], recv_sem=hop_recv.at[way, m],
            device_id=(to, me), device_id_type=MESH,
        )

    below = lax.rem(sec + 1, sections)
    above = lax.rem(sec + sections - 1, sections)

    @pl.when(sec < last)
    def _():
        low_copy(sec).start()

    for m in range(micro):
        ids_row, ids_col = id_row[m].astype(f32), id_col[m].astype(f32)
        same = jnp.where(ids_col == ids_row, 1.0, 0.0)
        first = lax.broadcasted_iota(jnp.int32, (rows, rows), 0)
        second = lax.broadcasted_iota(jnp.int32, (rows, rows), 1)
        rank_col = jnp.sum(jnp.where(second < first, same, 0.0), axis=1, keepdims=True)
        rank_row = jnp.sum(jnp.where(first < second, same, 0.0), axis=0, keepdims=True)
        grid_row = lax.broadcasted_iota(jnp.int32, (count, rows), 0).astype(f32)
        grid_col = lax.broadcasted_iota(jnp.int32, (rows, count), 1).astype(f32)
        spread[m] = jnp.where(grid_row == ids_row * slot + rank_row, 1.0, 0.0).astype(bf16)
        gather[m] = jnp.where(grid_col == ids_col * slot + rank_col, 1.0, 0.0).astype(bf16)

    @pl.when(sec == last)
    def _():
        @pl.loop(0, last)
        def _(source):
            low_copy(source).wait_recv()

        @pl.loop(1, experts)
        def _(k):
            low_spread(lax.rem(me + k, experts), me).start()

        low_all[last] = low[...]

    group = min(experts, 8)
    wide = group * slot

    def in_groups(run):
        if experts == group:
            run(pl.ds(0, group), pl.ds(0, wide))
        else:

            @pl.loop(0, experts // group)
            def _(turn):
                run(
                    pl.ds(pl.multiple_of(turn * group, group), group),
                    pl.ds(pl.multiple_of(turn * wide, wide), wide),
                )

    def place(m, values):
        def run(peers, lines):
            placed = mm(spread[m, lines], values).astype(bf16)
            outgoing[m, peers] = placed.reshape(group, slot, width)

        in_groups(run)

    for m in range(micro):
        @pl.when(sec == 0)
        def _():
            h_in[m] = feat[m]

        @pl.when(sec > 0)
        def _():
            hop(0, m, h_out, h_in, below).wait_recv()

        values = h_in[m].astype(f32)
        row_scale = rms_scale(values)
        scale[m] = row_scale
        place(m, (values * row_scale).astype(bf16))
        send_slots(0, m, slots)

    for m in range(micro):
        wait_slots(0, m, slots)
        wait_sent(0, m, slots)

        def serve(peers, lines):
            normed = slots[m, peers].reshape(wide, width)
            gate_pre = mm(normed, gate_w[...])
            up_pre = mm(normed, up_w[...])
            gate_sig = sigmoid(gate_pre)
            act = gate_pre * gate_sig
            inner = (act * up_pre).astype(bf16)
            served = mm(inner, down_w[...]).astype(bf16)
            outgoing[m, peers] = served.reshape(group, slot, width)
            gate_act[m, lines] = act
            hidden[m, lines] = inner
            gate_slope[m, lines] = up_pre * (gate_sig * (1.0 + gate_pre * (1.0 - gate_sig)))

        in_groups(serve)
        send_slots(1, m, back)

    for m in range(micro):
        wait_slots(1, m, back)
        picked = mm(gather[m], back[m].reshape(count, width))
        h_out[m] = (h_in[m].astype(f32) + gates[m] * picked).astype(bf16)

        @pl.when(sec < last)
        def _():
            hop(0, m, h_out, h_in, below).start()

    for m in range(micro):
        wait_sent(1, m, back)

        @pl.when(sec < last)
        def _():
            hop(0, m, h_out, h_in, below).wait_send()

    @pl.when(sec == last)
    def _():
        @pl.loop(1, experts)
        def _(k):
            peer = lax.rem(me + k, experts)
            low_spread(peer, peer).wait_recv()

        low_rows[last] = h_out[...].reshape(micro * rows, width)

        def forward(step, carry):
            layer = last - step
            values = low_rows[layer].astype(f32)
            row_scale = rms_scale(values)
            low_scale[layer] = row_scale
            inner_pre = mm((values * row_scale).astype(bf16), low_all[layer, 0])
            inner_sig = sigmoid(inner_pre)
            inner_act = (inner_pre * inner_sig).astype(bf16)
            low_act[layer] = inner_act
            low_slope[layer] = inner_sig * (1.0 + inner_pre * (1.0 - inner_sig))
            result = (values + mm(inner_act, low_all[layer, 1], NT)).astype(bf16)

            @pl.when(layer > 0)
            def _():
                low_rows[layer - 1] = result

            @pl.when(layer == 0)
            def _():
                low_grads[0] = result

            return carry

        lax.fori_loop(0, sections, forward, 0)
        values = low_grads[0].astype(f32)
        row_scale = rms_scale(values)
        logits = row_scale * jnp.sum(values * head[...], axis=1, keepdims=True)
        grad_logit = sigmoid(logits) - label[...].astype(f32)
        low_grads[0] = norm_back(values, row_scale, grad_logit * head[...]).astype(bf16)

        def backward(layer, carry):
            values = low_rows[layer].astype(f32)
            row_scale = low_scale[layer]
            grads = low_grads[layer]
            grad_pre = (mm(grads, low_all[layer, 1]) * low_slope[layer]).astype(bf16)
            low_pre[layer] = grad_pre
            grad_norm = mm(grad_pre, low_all[layer, 0], NT)
            result = (grads.astype(f32) + norm_back(values, row_scale, grad_norm)).astype(bf16)

            @pl.when(layer < last)
            def _():
                low_grads[layer + 1] = result

            @pl.when(layer == last)
            def _():
                g_in[...] = result.reshape(micro, rows, width)

            return carry

        lax.fori_loop(0, sections, backward, 0)

    for m in range(micro):
        @pl.when(sec < last)
        def _():
            hop(1, m, h_out, g_in, above).wait_recv()

        place(m, (gates[m] * g_in[m].astype(f32)).astype(bf16))
        send_slots(2, m, slot_grads)

    for m in range(micro):
        wait_slots(2, m, slot_grads)
        wait_sent(2, m, slot_grads)

        def slope(peers, lines):
            grad_hidden = mm(slot_grads[m, peers].reshape(wide, width), down_w[...], NT)
            grad_gate[m, lines] = (grad_hidden * gate_slope[m, lines]).astype(bf16)
            grad_up[m, lines] = (grad_hidden * gate_act[m, lines]).astype(bf16)

        in_groups(slope)

        @pl.when(sec > 0)
        def _():
            def answer(peers, lines):
                grad_slots = mm(grad_gate[m, lines], gate_w[...], NT) + mm(
                    grad_up[m, lines], up_w[...], NT
                )
                outgoing[m, peers] = grad_slots.astype(bf16).reshape(group, slot, width)

            in_groups(answer)
            send_slots(3, m, back)

    @pl.when(sec > 0)
    def _():
        for m in range(micro):
            wait_slots(3, m, back)
            picked = mm(gather[m], back[m].reshape(count, width))
            h_out[m] = (
                g_in[m].astype(f32) + norm_back(h_in[m].astype(f32), scale[m], picked)
            ).astype(bf16)
            hop(1, m, h_out, g_in, above).start()

        for m in range(micro):
            wait_sent(3, m, back)

    def share_copy(peer, owner):
        part = pl.ds(pl.multiple_of(peer * piece, piece), piece)
        return pltpu.make_async_remote_copy(
            src_ref=low_all.at[:, :, part, :], dst_ref=parts.at[owner],
            send_sem=p_send.at[peer], recv_sem=p_recv.at[owner],
            device_id=(sec, peer), device_id_type=MESH,
        )

    def share_out(section):
        return pltpu.make_async_remote_copy(
            src_ref=shares.at[section], dst_ref=share_in, send_sem=q_send.at[section],
            recv_sem=q_recv, device_id=(section, me), device_id_type=MESH,
        )

    @pl.when(sec == last)
    def _():
        @pl.loop(1, experts)
        def _(k):
            low_spread(lax.rem(me + k, experts), me).wait_send()

        def products(layer, carry):
            normed = (low_rows[layer].astype(f32) * low_scale[layer]).astype(bf16)
            low_all[layer, 0] = mm(normed, low_pre[layer], TN).astype(bf16)
            low_all[layer, 1] = mm(low_grads[layer], low_act[layer], TN).astype(bf16)
            return carry

        lax.fori_loop(0, sections, products, 0)

        @pl.loop(1, experts)
        def _(k):
            share_copy(lax.rem(me + k, experts), me).start()

    flat = micro * count
    step = stage.shape[-1]
    chunks = width // step

    def writes(chunk):
        cols = pl.ds(pl.multiple_of(chunk * step, step), step)
        at = lax.rem(chunk, 2)
        targets = (out_gate.at[cols, :], out_up.at[cols, :], out_down.at[:, cols])
        return [
            pltpu.make_async_copy(stage.at[at, kind], target, out_sem.at[at, kind])
            for kind, target in enumerate(targets)
        ]

    @pl.loop(0, chunks)
    def _(chunk):
        @pl.when(chunk >= 2)
        def _():
            for copy in writes(chunk - 2):
                copy.wait()

        cols = pl.ds(pl.multiple_of(chunk * step, step), step)
        at = lax.rem(chunk, 2)
        normed = slots[:, :, :, cols].reshape(flat, step)
        grads = slot_grads[:, :, :, cols].reshape(flat, step)
        stage[at, 0] = mm(normed, grad_gate[...].reshape(flat, -1), TN)
        stage[at, 1] = mm(normed, grad_up[...].reshape(flat, -1), TN)
        stage[at, 2] = mm(hidden[...].reshape(flat, -1), grads, TN)
        for copy in writes(chunk):
            copy.start()

    for chunk in range(max(0, chunks - 2), chunks):
        for copy in writes(chunk):
            copy.wait()

    @pl.when(sec == last)
    def _():
        @pl.loop(1, experts)
        def _(k):
            peer = lax.rem(me + k, experts)
            share_copy(peer, peer).wait_recv()

        def total(layer, carry):
            def add(k, acc):
                return acc + parts[lax.rem(me + k, experts), layer].astype(f32)

            acc = lax.fori_loop(1, experts, add, low_all[layer, :, mine, :].astype(f32))
            shares[layer] = acc.astype(bf16)
            return carry

        lax.fori_loop(0, sections, total, 0)

        @pl.loop(0, last)
        def _(section):
            share_out(section).start()

        out_low[...] = shares[last].astype(f32)

        @pl.loop(0, last)
        def _(section):
            share_out(section).wait_send()

        @pl.loop(1, experts)
        def _(k):
            share_copy(lax.rem(me + k, experts), me).wait_send()

    @pl.when(sec < last)
    def _():
        low_copy(sec).wait_send()
        share_out(last).wait_recv()
        out_low[...] = share_in[...].astype(f32)

    @pl.when(sec > 0)
    def _():
        for m in range(micro):
            hop(1, m, h_out, g_in, above).wait_send()


def local(
    sections, experts,
    features, labels, routes, route_gates, gate_weight, up_weight, down_weight,
    lowrank_in, lowrank_out, head_weight,
):
    micro, rows, width = features.shape
    hidden_width, rank = gate_weight.shape[-1], lowrank_in.shape[-1]
    capacity = min(rows, max(2, 3 * rows // (2 * experts)))
    slot = -(-capacity // TILE) * TILE
    count, piece, flat = experts * slot, width // experts, micro * rows
    low = jnp.stack([lowrank_in[0], lowrank_out[0].T])
    ids = routes.reshape(micro, rows)
    vmem = pl.BlockSpec(memory_space=pltpu.VMEM)
    dma = pltpu.SemaphoreType.DMA
    buffer = pltpu.VMEM((micro, experts, slot, width), bf16)
    row_buffer = pltpu.VMEM((micro, rows, width), bf16)
    inner = lambda kind: pltpu.VMEM((micro, count, hidden_width), kind)
    out = pl.pallas_call(
        functools.partial(kernel, sections, experts, slot),
        out_shape=(
            jax.ShapeDtypeStruct((width, hidden_width), f32),
            jax.ShapeDtypeStruct((width, hidden_width), f32),
            jax.ShapeDtypeStruct((hidden_width, width), f32),
            jax.ShapeDtypeStruct((2, piece, rank), f32),
        ),
        in_specs=[vmem] * 10,
        out_specs=(pl.BlockSpec(memory_space=pl.ANY),) * 3 + (vmem,),
        scratch_shapes=[
            row_buffer, row_buffer, row_buffer,
            pltpu.VMEM((micro, rows, 1), f32),
            pltpu.VMEM((micro, count, rows), bf16),
            pltpu.VMEM((micro, rows, count), bf16),
            buffer, buffer, buffer, buffer,
            inner(f32), inner(f32), inner(bf16), inner(bf16), inner(bf16),
            pltpu.VMEM((sections, 2, width, rank), bf16),
            pltpu.VMEM((sections, flat, width), bf16),
            pltpu.VMEM((sections, flat, width), bf16),
            pltpu.VMEM((sections, flat, 1), f32),
            pltpu.VMEM((sections, flat, rank), bf16),
            pltpu.VMEM((sections, flat, rank), f32),
            pltpu.VMEM((sections, flat, rank), bf16),
            pltpu.VMEM((experts, sections, 2, piece, rank), bf16),
            pltpu.VMEM((sections, 2, piece, rank), bf16),
            pltpu.VMEM((2, piece, rank), bf16),
            pltpu.VMEM((2, 3, hidden_width, hidden_width), f32), dma((2, 3)),
            dma((4, micro, experts)), dma((4, micro, experts)),
            dma((2, micro)), dma((2, micro)),
            dma, dma((sections,)),
            dma((experts,)), dma((experts,)),
            dma((experts,)), dma((experts,)),
            dma((sections,)), dma,
        ],
        compiler_params=pltpu.CompilerParams(
            collective_id=0, has_side_effects=True, vmem_limit_bytes=60 * 1024 * 1024
        ),
    )(
        features, labels.reshape(flat, 1), ids[:, None, :], ids[:, :, None],
        route_gates.reshape(micro, rows, 1), gate_weight[0, 0], up_weight[0, 0],
        down_weight[0, 0], low, head_weight[None, :],
    )
    return (
        out[0][None, None], out[1][None, None], out[2][None, None], out[3][0][None],
        out[3][1].T[None],
    )


def solution(mesh):
    return jax.shard_map(
        functools.partial(local, mesh.shape["section"], mesh.shape["expert"]),
        mesh=mesh,
        in_specs=(
            P(None, "expert", None),
            P(None, "expert"),
            P("section", None, "expert", None),
            P("section", None, "expert"),
            P("section", "expert", None, None),
            P("section", "expert", None, None),
            P("section", "expert", None, None),
            P("section", None, None),
            P("section", None, None),
            P(),
        ),
        out_specs=(
            P("section", "expert", None, None),
            P("section", "expert", None, None),
            P("section", "expert", None, None),
            P("section", "expert", None),
            P("section", None, "expert"),
        ),
        check_vma=False,
    )
```

```python
import functools

import jax
import jax.numpy as jnp
from jax import lax
from jax.experimental import pallas as pl
from jax.experimental.pallas import tpu as pltpu
from jax.sharding import PartitionSpec as P

epsilon = 1e-06
MESH = pl.DeviceIdType.MESH
f32, bf16 = jnp.float32, jnp.bfloat16
TILE = 16
NN = (((1,), (0,)), ((), ()))
NT = (((1,), (1,)), ((), ()))
TN = (((0,), (0,)), ((), ()))


def mm(left, right, dims=NN):
    return lax.dot_general(left, right, dims, preferred_element_type=f32)


def rms_scale(widened):
    return lax.rsqrt(jnp.mean(widened * widened, axis=-1, keepdims=True) + epsilon)


def norm_back(widened, row_scale, grad_norm):
    inner_mean = jnp.mean(grad_norm * widened, axis=-1, keepdims=True)
    return row_scale * grad_norm - widened * (row_scale * row_scale * row_scale) * inner_mean


def sigmoid(values):
    return jax.nn.sigmoid(values)


def kernel(
    sections, experts, slot,
    feat, label, ids, gate_row, gate_w, up_w, down_w, low_in, low_out, head,
    slots, slot_grads, hidden, grad_gate, grad_up, share_in,
    h_in, h_out, g_in, scale, gates, spread, gather, outgoing, back,
    gate_act, gate_slope,
    low, low_all, low_rows, low_grads, low_scale, low_act, low_slope, low_pre, parts, shares,
    x_send, x_recv, hop_send, hop_recv, lw_send, lw_recv, lb_send, lb_recv,
    p_send, p_recv, q_send, q_recv,
):
    micro, rows, width = feat.shape
    count = experts * slot
    piece = width // experts
    last = sections - 1
    sec, me = lax.axis_index("section"), lax.axis_index("expert")
    mine = pl.ds(pl.multiple_of(me * piece, piece), piece)

    barrier = pltpu.get_barrier_semaphore()

    @pl.loop(1, experts)
    def _(k):
        pl.semaphore_signal(
            barrier, inc=1, device_id=(sec, lax.rem(me + k, experts)), device_id_type=MESH
        )

    @pl.loop(1, sections)
    def _(k):
        pl.semaphore_signal(
            barrier, inc=1, device_id=(lax.rem(sec + k, sections), me), device_id_type=MESH
        )

    pl.semaphore_wait(barrier, experts + sections - 2)

    def low_copy(source):
        return pltpu.make_async_remote_copy(
            src_ref=low.at[:, mine, :], dst_ref=low_all.at[source, :, mine, :],
            send_sem=lw_send, recv_sem=lw_recv.at[source],
            device_id=(last, me), device_id_type=MESH,
        )

    def low_spread(peer, owner):
        part = pl.ds(pl.multiple_of(owner * piece, piece), piece)
        view = low_all.at[pl.ds(0, last), :, part, :]
        return pltpu.make_async_remote_copy(
            src_ref=view, dst_ref=view, send_sem=lb_send.at[peer], recv_sem=lb_recv.at[owner],
            device_id=(sec, peer), device_id_type=MESH,
        )

    def exchange(phase, m, peer, owner, target):
        return pltpu.make_async_remote_copy(
            src_ref=outgoing.at[m, peer], dst_ref=target.at[m, owner],
            send_sem=x_send.at[phase, m, peer], recv_sem=x_recv.at[phase, m, owner],
            device_id=(sec, peer), device_id_type=MESH,
        )

    def send_slots(phase, m, target):
        @pl.loop(1, experts)
        def _(k):
            exchange(phase, m, lax.rem(me + k, experts), me, target).start()

        target[m, me] = outgoing[m, me]

    def wait_slots(phase, m, target):
        @pl.loop(1, experts)
        def _(k):
            peer = lax.rem(me + k, experts)
            exchange(phase, m, peer, peer, target).wait_recv()

    def wait_sent(phase, m, target):
        @pl.loop(1, experts)
        def _(k):
            exchange(phase, m, lax.rem(me + k, experts), me, target).wait_send()

    def hop(way, m, source, target, to):
        return pltpu.make_async_remote_copy(
            src_ref=source.at[m], dst_ref=target.at[m],
            send_sem=hop_send.at[way, m], recv_sem=hop_recv.at[way, m],
            device_id=(to, me), device_id_type=MESH,
        )

    below = lax.rem(sec + 1, sections)
    above = lax.rem(sec + sections - 1, sections)

    def eye(size):
        first = lax.broadcasted_iota(jnp.int32, (size, size), 0)
        second = lax.broadcasted_iota(jnp.int32, (size, size), 1)
        return first, second

    def column(values):
        first, second = eye(values.shape[1])
        return jnp.sum(jnp.where(first == second, values, 0.0), axis=1, keepdims=True)

    def prepare_low():
        first, second = eye(low_out.shape[0])
        low[0] = low_in[...]
        low[1] = mm(low_out[...], jnp.where(first == second, 1.0, 0.0).astype(bf16), TN).astype(bf16)

        @pl.when(sec < last)
        def _():
            low_copy(sec).start()

    @pl.when(sec > 0)
    def _():
        prepare_low()

    def prepare_routes(m):
        ids_row = ids[m].astype(f32)
        ids_col = column(ids_row)
        same = jnp.where(ids_col == ids_row, 1.0, 0.0)
        first, second = eye(rows)
        rank_col = jnp.sum(jnp.where(second < first, same, 0.0), axis=1, keepdims=True)
        rank_row = jnp.sum(jnp.where(first < second, same, 0.0), axis=0, keepdims=True)
        grid_row = lax.broadcasted_iota(jnp.int32, (count, rows), 0).astype(f32)
        grid_col = lax.broadcasted_iota(jnp.int32, (rows, count), 1).astype(f32)
        spread[m] = jnp.where(grid_row == ids_row * slot + rank_row, 1.0, 0.0).astype(bf16)
        gather[m] = jnp.where(grid_col == ids_col * slot + rank_col, 1.0, 0.0).astype(bf16)
        gates[m] = column(gate_row[m])

    for m in range(micro):
        prepare_routes(m)

    @pl.when(sec == last)
    def _():
        @pl.loop(0, last)
        def _(source):
            low_copy(source).wait_recv()

        @pl.loop(1, experts)
        def _(k):
            low_spread(lax.rem(me + k, experts), me).start()

        low_all[last] = low[...]

    group = min(experts, 8)
    wide = group * slot

    def in_groups(run):
        if experts == group:
            run(pl.ds(0, group), pl.ds(0, wide))
        else:

            @pl.loop(0, experts // group)
            def _(turn):
                run(
                    pl.ds(pl.multiple_of(turn * group, group), group),
                    pl.ds(pl.multiple_of(turn * wide, wide), wide),
                )

    def place(m, values):
        def run(peers, lines):
            placed = mm(spread[m, lines], values).astype(bf16)
            outgoing[m, peers] = placed.reshape(group, slot, width)

        in_groups(run)

    def send_forward(m):
        @pl.when(sec == 0)
        def _():
            h_in[m] = feat[m]

        @pl.when(sec > 0)
        def _():
            hop(0, m, h_out, h_in, below).wait_recv()

        values = h_in[m].astype(f32)
        row_scale = rms_scale(values)
        scale[m] = row_scale
        place(m, (values * row_scale).astype(bf16))
        send_slots(0, m, slots)

    def serve_forward(m):
        wait_slots(0, m, slots)
        wait_sent(0, m, slots)

        def serve(peers, lines):
            normed = slots[m, peers].reshape(wide, width)
            gate_pre = mm(normed, gate_w[...])
            up_pre = mm(normed, up_w[...])
            gate_sig = sigmoid(gate_pre)
            act = gate_pre * gate_sig
            inner = (act * up_pre).astype(bf16)
            served = mm(inner, down_w[...]).astype(bf16)
            outgoing[m, peers] = served.reshape(group, slot, width)
            gate_act[m, lines] = act
            hidden[m, lines] = inner
            gate_slope[m, lines] = up_pre * (gate_sig * (1.0 + gate_pre * (1.0 - gate_sig)))

        in_groups(serve)
        send_slots(1, m, back)

    def end_forward(m):
        wait_slots(1, m, back)
        picked = mm(gather[m], back[m].reshape(count, width))
        h_out[m] = (h_in[m].astype(f32) + gates[m] * picked).astype(bf16)

        @pl.when(sec < last)
        def _():
            hop(0, m, h_out, h_in, below).start()

        wait_sent(1, m, back)

    def low_layers(m):
        low_rows[last, m] = h_out[m]

        def forward(step, carry):
            layer = last - step
            values = low_rows[layer, m].astype(f32)
            row_scale = rms_scale(values)
            low_scale[layer, m] = row_scale
            inner_pre = mm((values * row_scale).astype(bf16), low_all[layer, 0])
            inner_sig = sigmoid(inner_pre)
            inner_act = (inner_pre * inner_sig).astype(bf16)
            low_act[layer, m] = inner_act
            low_slope[layer, m] = inner_sig * (1.0 + inner_pre * (1.0 - inner_sig))
            result = (values + mm(inner_act, low_all[layer, 1], NT)).astype(bf16)

            @pl.when(layer > 0)
            def _():
                low_rows[layer - 1, m] = result

            @pl.when(layer == 0)
            def _():
                low_grads[0, m] = result

            return carry

        lax.fori_loop(0, sections, forward, 0)
        values = low_grads[0, m].astype(f32)
        row_scale = rms_scale(values)
        logits = row_scale * jnp.sum(values * head[...], axis=1, keepdims=True)
        grad_logit = sigmoid(logits) - column(label[m].astype(f32))
        low_grads[0, m] = norm_back(values, row_scale, grad_logit * head[...]).astype(bf16)

        def backward(layer, carry):
            values = low_rows[layer, m].astype(f32)
            row_scale = low_scale[layer, m]
            grads = low_grads[layer, m]
            grad_pre = (mm(grads, low_all[layer, 1]) * low_slope[layer, m]).astype(bf16)
            low_pre[layer, m] = grad_pre
            grad_norm = mm(grad_pre, low_all[layer, 0], NT)
            result = (grads.astype(f32) + norm_back(values, row_scale, grad_norm)).astype(bf16)

            @pl.when(layer < last)
            def _():
                low_grads[layer + 1, m] = result

            @pl.when(layer == last)
            def _():
                g_in[m] = result

            return carry

        lax.fori_loop(0, sections, backward, 0)

    def send_backward(m):
        place(m, (gates[m] * g_in[m].astype(f32)).astype(bf16))
        send_slots(2, m, slot_grads)

    def serve_backward(m):
        wait_slots(2, m, slot_grads)
        wait_sent(2, m, slot_grads)

        def slope(peers, lines):
            grad_hidden = mm(slot_grads[m, peers].reshape(wide, width), down_w[...], NT)
            grad_gate[m, lines] = (grad_hidden * gate_slope[m, lines]).astype(bf16)
            grad_up[m, lines] = (grad_hidden * gate_act[m, lines]).astype(bf16)

        in_groups(slope)

        @pl.when(sec > 0)
        def _():
            def answer(peers, lines):
                grad_slots = mm(grad_gate[m, lines], gate_w[...], NT) + mm(
                    grad_up[m, lines], up_w[...], NT
                )
                outgoing[m, peers] = grad_slots.astype(bf16).reshape(group, slot, width)

            in_groups(answer)
            send_slots(3, m, back)

    def end_backward(m):
        @pl.when(sec > 0)
        def _():
            wait_slots(3, m, back)
            picked = mm(gather[m], back[m].reshape(count, width))

            @pl.when(sec < last)
            def _():
                hop(0, m, h_out, h_in, below).wait_send()

            h_out[m] = (
                g_in[m].astype(f32) + norm_back(h_in[m].astype(f32), scale[m], picked)
            ).astype(bf16)
            hop(1, m, h_out, g_in, above).start()
            wait_sent(3, m, back)

        @pl.when(sec == 0)
        def _():
            hop(0, m, h_out, h_in, below).wait_send()

    send_forward(0)

    @pl.when(sec == 0)
    def _():
        prepare_low()

    for m in range(micro):
        if m:
            send_forward(m)

            @pl.when(sec == last)
            def _():
                if m == 1:
                    @pl.loop(1, experts)
                    def _(k):
                        peer = lax.rem(me + k, experts)
                        low_spread(peer, peer).wait_recv()

                low_layers(m - 1)
                send_backward(m - 1)

        serve_forward(m)
        if m:
            @pl.when(sec == last)
            def _():
                serve_backward(m - 1)

        end_forward(m)
        if m > 1:
            @pl.when(sec == last)
            def _():
                end_backward(m - 2)

    final = micro - 1

    @pl.when(sec == last)
    def _():
        if micro == 1:
            @pl.loop(1, experts)
            def _(k):
                peer = lax.rem(me + k, experts)
                low_spread(peer, peer).wait_recv()

        low_layers(final)
        send_backward(final)
        if micro > 1:
            end_backward(final - 1)
        serve_backward(final)
        end_backward(final)

    @pl.when(sec < last)
    def _():
        for m in range(micro):
            hop(1, m, h_out, g_in, above).wait_recv()
            send_backward(m)
            serve_backward(m)
            end_backward(m)

    def share_copy(peer, owner):
        part = pl.ds(pl.multiple_of(peer * piece, piece), piece)
        return pltpu.make_async_remote_copy(
            src_ref=low_all.at[:, :, part, :], dst_ref=parts.at[owner],
            send_sem=p_send.at[peer], recv_sem=p_recv.at[owner],
            device_id=(sec, peer), device_id_type=MESH,
        )

    def share_out(section):
        return pltpu.make_async_remote_copy(
            src_ref=shares.at[section], dst_ref=share_in, send_sem=q_send.at[section],
            recv_sem=q_recv, device_id=(section, me), device_id_type=MESH,
        )

    @pl.when(sec == last)
    def _():
        @pl.loop(1, experts)
        def _(k):
            low_spread(lax.rem(me + k, experts), me).wait_send()

        def products(layer, carry):
            normed = (low_rows[layer].astype(f32) * low_scale[layer]).astype(bf16)
            normed = normed.reshape(micro * rows, width)
            grads = low_grads[layer].reshape(micro * rows, width)
            pre = low_pre[layer].reshape(micro * rows, -1)
            act = low_act[layer].reshape(micro * rows, -1)
            low_all[layer, 0] = mm(normed, pre, TN).astype(bf16)
            low_all[layer, 1] = mm(grads, act, TN).astype(bf16)
            return carry

        lax.fori_loop(0, sections, products, 0)

        @pl.loop(1, experts)
        def _(k):
            share_copy(lax.rem(me + k, experts), me).start()

    @pl.when(sec == last)
    def _():
        @pl.loop(1, experts)
        def _(k):
            peer = lax.rem(me + k, experts)
            share_copy(peer, peer).wait_recv()

        def total(layer, carry):
            def add(k, acc):
                return acc + parts[lax.rem(me + k, experts), layer].astype(f32)

            acc = lax.fori_loop(1, experts, add, low_all[layer, :, mine, :].astype(f32))
            shares[layer] = acc.astype(bf16)
            return carry

        lax.fori_loop(0, sections, total, 0)

        @pl.loop(0, last)
        def _(section):
            share_out(section).start()

        share_in[...] = shares[last]

        @pl.loop(0, last)
        def _(section):
            share_out(section).wait_send()

        @pl.loop(1, experts)
        def _(k):
            share_copy(lax.rem(me + k, experts), me).wait_send()

    @pl.when(sec < last)
    def _():
        low_copy(sec).wait_send()
        share_out(last).wait_recv()

    @pl.when(sec > 0)
    def _():
        for m in range(micro):
            hop(1, m, h_out, g_in, above).wait_send()


def products_kernel(
    slots, slot_grads, hidden, grad_gate, grad_up, share,
    out_gate, out_up, out_down, out_in, out_out,
):
    out_gate[...] = mm(slots[...], grad_gate[...], TN)
    out_up[...] = mm(slots[...], grad_up[...], TN)
    out_down[...] = mm(hidden[...], slot_grads[...], TN)

    @pl.when(pl.program_id(0) == 0)
    def _():
        out_in[...] = share[0].astype(f32)
        size = share.shape[2]
        first = lax.broadcasted_iota(jnp.int32, (size, size), 0)
        second = lax.broadcasted_iota(jnp.int32, (size, size), 1)
        unit = jnp.where(first == second, 1.0, 0.0).astype(bf16)
        out_out[...] = mm(unit, share[1], NT)


def local(
    sections, experts,
    features, labels, routes, route_gates, gate_weight, up_weight, down_weight,
    lowrank_in, lowrank_out, head_weight,
):
    micro, rows, width = features.shape
    inner_width, rank = gate_weight.shape[-1], lowrank_in.shape[-1]
    capacity = min(rows, max(2, 3 * rows // (2 * experts)))
    slot = -(-capacity // TILE) * TILE
    count, piece = experts * slot, width // experts
    flat = micro * count
    vmem = pl.BlockSpec(memory_space=pltpu.VMEM)
    dma = pltpu.SemaphoreType.DMA
    buffer = pltpu.VMEM((micro, experts, slot, width), bf16)
    row_buffer = pltpu.VMEM((micro, rows, width), bf16)
    slot_shape = jax.ShapeDtypeStruct((micro, experts, slot, width), bf16)
    inner_shape = jax.ShapeDtypeStruct((micro, count, inner_width), bf16)
    inner = pltpu.VMEM((micro, count, inner_width), f32)
    low_buffer = pltpu.VMEM((sections, micro, rows, width), bf16)
    made = pl.pallas_call(
        functools.partial(kernel, sections, experts, slot),
        out_shape=(
            slot_shape, slot_shape, inner_shape, inner_shape, inner_shape,
            jax.ShapeDtypeStruct((2, piece, rank), bf16),
        ),
        in_specs=[vmem] * 10,
        out_specs=(vmem,) * 6,
        scratch_shapes=[
            row_buffer, row_buffer, row_buffer,
            pltpu.VMEM((micro, rows, 1), f32),
            pltpu.VMEM((micro, rows, 1), f32),
            pltpu.VMEM((micro, count, rows), bf16),
            pltpu.VMEM((micro, rows, count), bf16),
            buffer, buffer, inner, inner,
            pltpu.VMEM((2, width, rank), bf16),
            pltpu.VMEM((sections, 2, width, rank), bf16),
            low_buffer, low_buffer,
            pltpu.VMEM((sections, micro, rows, 1), f32),
            pltpu.VMEM((sections, micro, rows, rank), bf16),
            pltpu.VMEM((sections, micro, rows, rank), f32),
            pltpu.VMEM((sections, micro, rows, rank), bf16),
            pltpu.VMEM((experts, sections, 2, piece, rank), bf16),
            pltpu.VMEM((sections, 2, piece, rank), bf16),
            dma((4, micro, experts)), dma((4, micro, experts)),
            dma((2, micro)), dma((2, micro)),
            dma, dma((sections,)),
            dma((experts,)), dma((experts,)),
            dma((experts,)), dma((experts,)),
            dma((sections,)), dma,
        ],
        compiler_params=pltpu.CompilerParams(
            collective_id=0, has_side_effects=True, vmem_limit_bytes=60 * 1024 * 1024
        ),
    )(
        features, labels.reshape(micro, 1, rows), routes.reshape(micro, 1, rows),
        route_gates.reshape(micro, 1, rows), gate_weight[0, 0], up_weight[0, 0],
        down_weight[0, 0], lowrank_in[0], lowrank_out[0], head_weight[None, :],
    )
    slots, slot_grads, hidden, grad_gate, grad_up, share = made
    step = min(width, 512)
    wide = pl.BlockSpec((flat, step), lambda i: (0, i))
    narrow = pl.BlockSpec((flat, inner_width), lambda i: (0, 0))
    tall = pl.BlockSpec((step, inner_width), lambda i: (i, 0))
    outs = pl.pallas_call(
        products_kernel,
        grid=(width // step,),
        out_shape=(
            jax.ShapeDtypeStruct((width, inner_width), f32),
            jax.ShapeDtypeStruct((width, inner_width), f32),
            jax.ShapeDtypeStruct((inner_width, width), f32),
            jax.ShapeDtypeStruct((piece, rank), f32),
            jax.ShapeDtypeStruct((rank, piece), f32),
        ),
        in_specs=[
            wide, wide, narrow, narrow, narrow,
            pl.BlockSpec((2, piece, rank), lambda i: (0, 0, 0)),
        ],
        out_specs=(
            tall, tall, pl.BlockSpec((inner_width, step), lambda i: (0, i)),
            pl.BlockSpec((piece, rank), lambda i: (0, 0)),
            pl.BlockSpec((rank, piece), lambda i: (0, 0)),
        ),
        compiler_params=pltpu.CompilerParams(vmem_limit_bytes=32 * 1024 * 1024),
    )(
        slots.reshape(flat, width), slot_grads.reshape(flat, width),
        hidden.reshape(flat, inner_width), grad_gate.reshape(flat, inner_width),
        grad_up.reshape(flat, inner_width), share,
    )
    return (
        outs[0][None, None], outs[1][None, None], outs[2][None, None], outs[3][None],
        outs[4][None],
    )


def solution(mesh):
    return jax.shard_map(
        functools.partial(local, mesh.shape["section"], mesh.shape["expert"]),
        mesh=mesh,
        in_specs=(
            P(None, "expert", None),
            P(None, "expert"),
            P("section", None, "expert", None),
            P("section", None, "expert"),
            P("section", "expert", None, None),
            P("section", "expert", None, None),
            P("section", "expert", None, None),
            P("section", None, None),
            P("section", None, None),
            P(),
        ),
        out_specs=(
            P("section", "expert", None, None),
            P("section", "expert", None, None),
            P("section", "expert", None, None),
            P("section", "expert", None),
            P("section", None, "expert"),
        ),
        check_vma=False,
    )
```

```python
import functools

import jax
import jax.numpy as jnp
from jax import lax
from jax.experimental import pallas as pl
from jax.experimental.pallas import tpu as pltpu
from jax.sharding import PartitionSpec as P

epsilon = 1e-06
MESH = pl.DeviceIdType.MESH
f32, bf16 = jnp.float32, jnp.bfloat16
TILE = 16
PIECES = 4
NN = (((1,), (0,)), ((), ()))
NT = (((1,), (1,)), ((), ()))
TN = (((0,), (0,)), ((), ()))


def mm(left, right, dims=NN):
    return lax.dot_general(left, right, dims, preferred_element_type=f32)


def rms_scale(widened):
    return lax.rsqrt(jnp.mean(widened * widened, axis=-1, keepdims=True) + epsilon)


def columns_of(values, piece, at):
    return values[:, at * piece : (at + 1) * piece]


def norm_back(widened, row_scale, grad_norm):
    inner_mean = jnp.mean(grad_norm * widened, axis=-1, keepdims=True)
    return row_scale * grad_norm - widened * (row_scale * row_scale * row_scale) * inner_mean


def sigmoid(values):
    return jax.nn.sigmoid(values)


def kernel(
    sections, experts, slot,
    feat, label, ids, gate_row, gate_w, up_w, down_w, low_in, low_out, head,
    slots, slot_scale, slot_grads, hidden, grad_gate, grad_up, share_in,
    h_in, h_out, g_in, gates, spread, gather, outgoing, back,
    gate_act, gate_slope,
    low, low_all, low_rows, low_grads, low_scale, low_act, low_slope, low_pre, parts, shares,
    x_send, x_recv, hop_send, hop_recv, lw_send, lw_recv, lb_send, lb_recv,
    p_send, p_recv, q_send, q_recv,
):
    micro, rows, width = feat.shape
    count = experts * slot
    piece = width // experts
    part_width = width // PIECES
    last = sections - 1
    sec, me = lax.axis_index("section"), lax.axis_index("expert")
    mine = pl.ds(pl.multiple_of(me * piece, piece), piece)

    barrier = pltpu.get_barrier_semaphore()

    @pl.loop(1, experts)
    def _(k):
        pl.semaphore_signal(
            barrier, inc=1, device_id=(sec, lax.rem(me + k, experts)), device_id_type=MESH
        )

    @pl.loop(1, sections)
    def _(k):
        pl.semaphore_signal(
            barrier, inc=1, device_id=(lax.rem(sec + k, sections), me), device_id_type=MESH
        )

    pl.semaphore_wait(barrier, experts + sections - 2)

    def low_copy(source):
        return pltpu.make_async_remote_copy(
            src_ref=low.at[:, mine, :], dst_ref=low_all.at[source, :, mine, :],
            send_sem=lw_send, recv_sem=lw_recv.at[source],
            device_id=(last, me), device_id_type=MESH,
        )

    def low_spread(peer, owner):
        part = pl.ds(pl.multiple_of(owner * piece, piece), piece)
        view = low_all.at[pl.ds(0, last), :, part, :]
        return pltpu.make_async_remote_copy(
            src_ref=view, dst_ref=view, send_sem=lb_send.at[peer], recv_sem=lb_recv.at[owner],
            device_id=(sec, peer), device_id_type=MESH,
        )

    def exchange(phase, m, c, peer, owner, target):
        return pltpu.make_async_remote_copy(
            src_ref=outgoing.at[m, c, peer], dst_ref=target.at[m, c, owner],
            send_sem=x_send.at[phase, m, c, peer], recv_sem=x_recv.at[phase, m, c, owner],
            device_id=(sec, peer), device_id_type=MESH,
        )

    def send_slots(phase, m, c, target):
        @pl.loop(1, experts)
        def _(k):
            exchange(phase, m, c, lax.rem(me + k, experts), me, target).start()

        target[m, c, me] = outgoing[m, c, me]

    def wait_slots(phase, m, c, target):
        @pl.loop(1, experts)
        def _(k):
            peer = lax.rem(me + k, experts)
            exchange(phase, m, c, peer, peer, target).wait_recv()

    def wait_sent(phase, m, c, target):
        @pl.loop(1, experts)
        def _(k):
            exchange(phase, m, c, lax.rem(me + k, experts), me, target).wait_send()

    def hop(way, m, c, source, target, to):
        return pltpu.make_async_remote_copy(
            src_ref=source.at[m, c], dst_ref=target.at[m, c],
            send_sem=hop_send.at[way, m, c], recv_sem=hop_recv.at[way, m, c],
            device_id=(to, me), device_id_type=MESH,
        )

    below = lax.rem(sec + 1, sections)
    above = lax.rem(sec + sections - 1, sections)

    def eye(size):
        first = lax.broadcasted_iota(jnp.int32, (size, size), 0)
        second = lax.broadcasted_iota(jnp.int32, (size, size), 1)
        return first, second

    def column(values):
        first, second = eye(values.shape[1])
        return jnp.sum(jnp.where(first == second, values, 0.0), axis=1, keepdims=True)

    def prepare_low():
        first, second = eye(low_out.shape[0])
        low[0] = low_in[...]
        low[1] = mm(low_out[...], jnp.where(first == second, 1.0, 0.0).astype(bf16), TN).astype(bf16)

        @pl.when(sec < last)
        def _():
            low_copy(sec).start()

    @pl.when(sec > 0)
    def _():
        prepare_low()

    def prepare_routes(m):
        ids_row = ids[m].astype(f32)
        ids_col = column(ids_row)
        same = jnp.where(ids_col == ids_row, 1.0, 0.0)
        first, second = eye(rows)
        rank_col = jnp.sum(jnp.where(second < first, same, 0.0), axis=1, keepdims=True)
        rank_row = jnp.sum(jnp.where(first < second, same, 0.0), axis=0, keepdims=True)
        grid_row = lax.broadcasted_iota(jnp.int32, (count, rows), 0).astype(f32)
        grid_col = lax.broadcasted_iota(jnp.int32, (rows, count), 1).astype(f32)
        spread[m] = jnp.where(grid_row == ids_row * slot + rank_row, 1.0, 0.0).astype(bf16)
        gather[m] = jnp.where(grid_col == ids_col * slot + rank_col, 1.0, 0.0).astype(bf16)
        gates[m] = column(gate_row[m])

    for m in range(micro):
        prepare_routes(m)

    @pl.when(sec == last)
    def _():
        @pl.loop(0, last)
        def _(source):
            low_copy(source).wait_recv()

        @pl.loop(1, experts)
        def _(k):
            low_spread(lax.rem(me + k, experts), me).start()

        low_all[last] = low[...]

    group = min(experts, 8)
    wide = group * slot

    def in_groups(run):
        if experts == group:
            run(pl.ds(0, group), pl.ds(0, wide))
        else:

            @pl.loop(0, experts // group)
            def _(turn):
                run(
                    pl.ds(pl.multiple_of(turn * group, group), group),
                    pl.ds(pl.multiple_of(turn * wide, wide), wide),
                )

    def place(m, c, values):
        def run(peers, lines):
            placed = mm(spread[m, lines], values).astype(bf16)
            outgoing[m, c, peers] = placed.reshape(group, slot, part_width)

        in_groups(run)

    def cols(c):
        return pl.ds(c * part_width, part_width)

    def lines_of(buffer, m, c, peers):
        return buffer[m, c, peers].reshape(wide, part_width)

    def send_forward(m):
        for c in range(PIECES):
            @pl.when(sec == 0)
            def _():
                h_in[m, c] = feat[m, :, cols(c)]

            @pl.when(sec > 0)
            def _():
                hop(0, m, c, h_out, h_in, below).wait_recv()

            place(m, c, h_in[m, c])
            send_slots(0, m, c, slots)

    def serve_forward(m):
        for c in range(PIECES):
            wait_slots(0, m, c, slots)

        def inward(peers, lines):
            total = 0.0
            for c in range(PIECES):
                values = lines_of(slots, m, c, peers).astype(f32)
                total = total + jnp.sum(values * values, axis=-1, keepdims=True)
            row_scale = lax.rsqrt(total / width + epsilon)
            slot_scale[m, lines] = row_scale
            gate_pre, up_pre = 0.0, 0.0
            for c in range(PIECES):
                values = lines_of(slots, m, c, peers).astype(f32)
                normed = (values * row_scale).astype(bf16)
                gate_pre = gate_pre + mm(normed, gate_w[cols(c), :])
                up_pre = up_pre + mm(normed, up_w[cols(c), :])
            gate_sig = sigmoid(gate_pre)
            act = gate_pre * gate_sig
            gate_act[m, lines] = act
            hidden[m, lines] = (act * up_pre).astype(bf16)
            gate_slope[m, lines] = up_pre * (gate_sig * (1.0 + gate_pre * (1.0 - gate_sig)))

        in_groups(inward)
        for c in range(PIECES):
            wait_sent(0, m, c, slots)

            def outward(peers, lines):
                served = mm(hidden[m, lines], down_w[:, cols(c)]).astype(bf16)
                outgoing[m, c, peers] = served.reshape(group, slot, part_width)

            in_groups(outward)
            send_slots(1, m, c, back)

    def end_forward(m):
        for c in range(PIECES):
            wait_slots(1, m, c, back)
            picked = mm(gather[m], back[m, c].reshape(count, part_width))
            h_out[m, c] = (h_in[m, c].astype(f32) + gates[m] * picked).astype(bf16)

            @pl.when(sec < last)
            def _():
                hop(0, m, c, h_out, h_in, below).start()

        for c in range(PIECES):
            wait_sent(1, m, c, back)

    def low_layers(m):
        for c in range(PIECES):
            low_rows[last, m, :, cols(c)] = h_out[m, c]

        def forward(step, carry):
            layer = last - step
            values = low_rows[layer, m].astype(f32)
            row_scale = rms_scale(values)
            low_scale[layer, m] = row_scale
            inner_pre = mm((values * row_scale).astype(bf16), low_all[layer, 0])
            inner_sig = sigmoid(inner_pre)
            inner_act = (inner_pre * inner_sig).astype(bf16)
            low_act[layer, m] = inner_act
            low_slope[layer, m] = inner_sig * (1.0 + inner_pre * (1.0 - inner_sig))
            result = (values + mm(inner_act, low_all[layer, 1], NT)).astype(bf16)

            @pl.when(layer > 0)
            def _():
                low_rows[layer - 1, m] = result

            @pl.when(layer == 0)
            def _():
                low_grads[0, m] = result

            return carry

        lax.fori_loop(0, sections, forward, 0)
        values = low_grads[0, m].astype(f32)
        row_scale = rms_scale(values)
        logits = row_scale * jnp.sum(values * head[...], axis=1, keepdims=True)
        grad_logit = sigmoid(logits) - column(label[m].astype(f32))
        low_grads[0, m] = norm_back(values, row_scale, grad_logit * head[...]).astype(bf16)

        def backward(layer, carry):
            values = low_rows[layer, m].astype(f32)
            row_scale = low_scale[layer, m]
            grads = low_grads[layer, m]
            grad_pre = (mm(grads, low_all[layer, 1]) * low_slope[layer, m]).astype(bf16)
            low_pre[layer, m] = grad_pre
            grad_norm = mm(grad_pre, low_all[layer, 0], NT)
            result = (grads.astype(f32) + norm_back(values, row_scale, grad_norm)).astype(bf16)

            @pl.when(layer < last)
            def _():
                low_grads[layer + 1, m] = result

            @pl.when(layer == last)
            def _():
                for c in range(PIECES):
                    g_in[m, c] = columns_of(result, part_width, c)

            return carry

        lax.fori_loop(0, sections, backward, 0)

    def send_backward(m):
        for c in range(PIECES):
            @pl.when(sec < last)
            def _():
                hop(1, m, c, h_out, g_in, above).wait_recv()

            place(m, c, (gates[m] * g_in[m, c].astype(f32)).astype(bf16))
            send_slots(2, m, c, slot_grads)

    def serve_backward(m):
        for c in range(PIECES):
            wait_slots(2, m, c, slot_grads)

        def slope(peers, lines):
            grad_hidden = 0.0
            for c in range(PIECES):
                grads = lines_of(slot_grads, m, c, peers)
                grad_hidden = grad_hidden + mm(grads, down_w[:, cols(c)], NT)
            grad_gate[m, lines] = (grad_hidden * gate_slope[m, lines]).astype(bf16)
            grad_up[m, lines] = (grad_hidden * gate_act[m, lines]).astype(bf16)

        in_groups(slope)
        for c in range(PIECES):
            wait_sent(2, m, c, slot_grads)

        @pl.when(sec > 0)
        def _():
            def answer(peers, lines):
                row_scale = slot_scale[m, lines]
                products, total = [], 0.0
                for c in range(PIECES):
                    grads = mm(grad_gate[m, lines], gate_w[cols(c), :], NT) + mm(
                        grad_up[m, lines], up_w[cols(c), :], NT
                    )
                    values = lines_of(slots, m, c, peers).astype(f32)
                    total = total + jnp.sum(grads * values, axis=-1, keepdims=True)
                    products.append(grads)
                weight = row_scale * row_scale * row_scale * (total / width)
                for c in range(PIECES):
                    values = lines_of(slots, m, c, peers).astype(f32)
                    result = (row_scale * products[c] - values * weight).astype(bf16)
                    outgoing[m, c, peers] = result.reshape(group, slot, part_width)

            in_groups(answer)
            for c in range(PIECES):
                send_slots(3, m, c, back)

    def end_backward(m):
        @pl.when(sec > 0)
        def _():
            for c in range(PIECES):
                wait_slots(3, m, c, back)
                picked = mm(gather[m], back[m, c].reshape(count, part_width))

                @pl.when(sec < last)
                def _():
                    hop(0, m, c, h_out, h_in, below).wait_send()

                h_out[m, c] = (g_in[m, c].astype(f32) + picked).astype(bf16)
                hop(1, m, c, h_out, g_in, above).start()

            for c in range(PIECES):
                wait_sent(3, m, c, back)

        @pl.when(sec == 0)
        def _():
            for c in range(PIECES):
                hop(0, m, c, h_out, h_in, below).wait_send()

    send_forward(0)

    @pl.when(sec == 0)
    def _():
        prepare_low()

    for m in range(micro):
        if m:
            send_forward(m)

            @pl.when(sec == last)
            def _():
                if m == 1:
                    @pl.loop(1, experts)
                    def _(k):
                        peer = lax.rem(me + k, experts)
                        low_spread(peer, peer).wait_recv()

                low_layers(m - 1)
                send_backward(m - 1)

        serve_forward(m)
        if m:
            @pl.when(sec == last)
            def _():
                serve_backward(m - 1)

        end_forward(m)
        if m > 1:
            @pl.when(sec == last)
            def _():
                end_backward(m - 2)

    final = micro - 1

    @pl.when(sec == last)
    def _():
        if micro == 1:
            @pl.loop(1, experts)
            def _(k):
                peer = lax.rem(me + k, experts)
                low_spread(peer, peer).wait_recv()

        low_layers(final)
        send_backward(final)
        if micro > 1:
            end_backward(final - 1)
        serve_backward(final)
        end_backward(final)

    @pl.when(sec < last)
    def _():
        for m in range(micro):
            send_backward(m)
            serve_backward(m)
            end_backward(m)

    def share_copy(peer, owner):
        part = pl.ds(pl.multiple_of(peer * piece, piece), piece)
        return pltpu.make_async_remote_copy(
            src_ref=low_all.at[:, :, part, :], dst_ref=parts.at[owner],
            send_sem=p_send.at[peer], recv_sem=p_recv.at[owner],
            device_id=(sec, peer), device_id_type=MESH,
        )

    def share_out(section):
        return pltpu.make_async_remote_copy(
            src_ref=shares.at[section], dst_ref=share_in, send_sem=q_send.at[section],
            recv_sem=q_recv, device_id=(section, me), device_id_type=MESH,
        )

    @pl.when(sec == last)
    def _():
        @pl.loop(1, experts)
        def _(k):
            low_spread(lax.rem(me + k, experts), me).wait_send()

        def products(layer, carry):
            normed = (low_rows[layer].astype(f32) * low_scale[layer]).astype(bf16)
            normed = normed.reshape(micro * rows, width)
            grads = low_grads[layer].reshape(micro * rows, width)
            pre = low_pre[layer].reshape(micro * rows, -1)
            act = low_act[layer].reshape(micro * rows, -1)
            low_all[layer, 0] = mm(normed, pre, TN).astype(bf16)
            low_all[layer, 1] = mm(grads, act, TN).astype(bf16)
            return carry

        lax.fori_loop(0, sections, products, 0)

        @pl.loop(1, experts)
        def _(k):
            share_copy(lax.rem(me + k, experts), me).start()

    @pl.when(sec == last)
    def _():
        @pl.loop(1, experts)
        def _(k):
            peer = lax.rem(me + k, experts)
            share_copy(peer, peer).wait_recv()

        def total(layer, carry):
            def add(k, acc):
                return acc + parts[lax.rem(me + k, experts), layer].astype(f32)

            acc = lax.fori_loop(1, experts, add, low_all[layer, :, mine, :].astype(f32))
            shares[layer] = acc.astype(bf16)
            return carry

        lax.fori_loop(0, sections, total, 0)

        @pl.loop(0, last)
        def _(section):
            share_out(section).start()

        share_in[...] = shares[last]

        @pl.loop(0, last)
        def _(section):
            share_out(section).wait_send()

        @pl.loop(1, experts)
        def _(k):
            share_copy(lax.rem(me + k, experts), me).wait_send()

    @pl.when(sec < last)
    def _():
        low_copy(sec).wait_send()
        share_out(last).wait_recv()

    @pl.when(sec > 0)
    def _():
        for m in range(micro):
            for c in range(PIECES):
                hop(1, m, c, h_out, g_in, above).wait_send()


def products_kernel(
    slots, scale, slot_grads, hidden, grad_gate, grad_up, share,
    out_gate, out_up, out_down, out_in, out_out,
):
    flat = hidden.shape[0]
    values = slots[...].reshape(flat, -1).astype(f32)
    normed = (values * scale[...].reshape(flat, 1)).astype(bf16)
    out_gate[...] = mm(normed, grad_gate[...], TN)
    out_up[...] = mm(normed, grad_up[...], TN)
    out_down[...] = mm(hidden[...], slot_grads[...].reshape(flat, -1), TN)

    @pl.when(pl.program_id(0) == 0)
    def _():
        out_in[...] = share[0].astype(f32)
        size = share.shape[2]
        first = lax.broadcasted_iota(jnp.int32, (size, size), 0)
        second = lax.broadcasted_iota(jnp.int32, (size, size), 1)
        unit = jnp.where(first == second, 1.0, 0.0).astype(bf16)
        out_out[...] = mm(unit, share[1], NT)


def local(
    sections, experts,
    features, labels, routes, route_gates, gate_weight, up_weight, down_weight,
    lowrank_in, lowrank_out, head_weight,
):
    micro, rows, width = features.shape
    inner_width, rank = gate_weight.shape[-1], lowrank_in.shape[-1]
    capacity = min(rows, max(2, 3 * rows // (2 * experts)))
    slot = -(-capacity // TILE) * TILE
    count, piece = experts * slot, width // experts
    flat = micro * count
    vmem = pl.BlockSpec(memory_space=pltpu.VMEM)
    dma = pltpu.SemaphoreType.DMA
    step = width // PIECES
    buffer = pltpu.VMEM((micro, PIECES, experts, slot, step), bf16)
    row_buffer = pltpu.VMEM((micro, PIECES, rows, step), bf16)
    slot_shape = jax.ShapeDtypeStruct((micro, PIECES, experts, slot, step), bf16)
    inner_shape = jax.ShapeDtypeStruct((micro, count, inner_width), bf16)
    inner = pltpu.VMEM((micro, count, inner_width), f32)
    low_buffer = pltpu.VMEM((sections, micro, rows, width), bf16)
    made = pl.pallas_call(
        functools.partial(kernel, sections, experts, slot),
        out_shape=(
            slot_shape, jax.ShapeDtypeStruct((micro, count, 1), f32), slot_shape, inner_shape, inner_shape, inner_shape,
            jax.ShapeDtypeStruct((2, piece, rank), bf16),
        ),
        in_specs=[vmem] * 10,
        out_specs=(vmem,) * 7,
        scratch_shapes=[
            row_buffer, row_buffer, row_buffer,
            pltpu.VMEM((micro, rows, 1), f32),
            pltpu.VMEM((micro, count, rows), bf16),
            pltpu.VMEM((micro, rows, count), bf16),
            buffer, buffer, inner, inner,
            pltpu.VMEM((2, width, rank), bf16),
            pltpu.VMEM((sections, 2, width, rank), bf16),
            low_buffer, low_buffer,
            pltpu.VMEM((sections, micro, rows, 1), f32),
            pltpu.VMEM((sections, micro, rows, rank), bf16),
            pltpu.VMEM((sections, micro, rows, rank), f32),
            pltpu.VMEM((sections, micro, rows, rank), bf16),
            pltpu.VMEM((experts, sections, 2, piece, rank), bf16),
            pltpu.VMEM((sections, 2, piece, rank), bf16),
            dma((4, micro, PIECES, experts)), dma((4, micro, PIECES, experts)),
            dma((2, micro, PIECES)), dma((2, micro, PIECES)),
            dma, dma((sections,)),
            dma((experts,)), dma((experts,)),
            dma((experts,)), dma((experts,)),
            dma((sections,)), dma,
        ],
        compiler_params=pltpu.CompilerParams(
            collective_id=0, has_side_effects=True, vmem_limit_bytes=60 * 1024 * 1024
        ),
    )(
        features, labels.reshape(micro, 1, rows), routes.reshape(micro, 1, rows),
        route_gates.reshape(micro, 1, rows), gate_weight[0, 0], up_weight[0, 0],
        down_weight[0, 0], lowrank_in[0], lowrank_out[0], head_weight[None, :],
    )
    slots, scale, slot_grads, hidden, grad_gate, grad_up, share = made
    wide = pl.BlockSpec((micro, 1, count, step), lambda i: (0, i, 0, 0))
    narrow = pl.BlockSpec((flat, inner_width), lambda i: (0, 0))
    tall = pl.BlockSpec((step, inner_width), lambda i: (i, 0))
    outs = pl.pallas_call(
        products_kernel,
        grid=(PIECES,),
        out_shape=(
            jax.ShapeDtypeStruct((width, inner_width), f32),
            jax.ShapeDtypeStruct((width, inner_width), f32),
            jax.ShapeDtypeStruct((inner_width, width), f32),
            jax.ShapeDtypeStruct((piece, rank), f32),
            jax.ShapeDtypeStruct((rank, piece), f32),
        ),
        in_specs=[
            wide, pl.BlockSpec((micro, count, 1), lambda i: (0, 0, 0)), wide, narrow, narrow, narrow,
            pl.BlockSpec((2, piece, rank), lambda i: (0, 0, 0)),
        ],
        out_specs=(
            tall, tall, pl.BlockSpec((inner_width, step), lambda i: (0, i)),
            pl.BlockSpec((piece, rank), lambda i: (0, 0)),
            pl.BlockSpec((rank, piece), lambda i: (0, 0)),
        ),
        compiler_params=pltpu.CompilerParams(vmem_limit_bytes=60 * 1024 * 1024),
    )(
        slots.reshape(micro, PIECES, count, step), scale,
        slot_grads.reshape(micro, PIECES, count, step),
        hidden.reshape(flat, inner_width), grad_gate.reshape(flat, inner_width),
        grad_up.reshape(flat, inner_width), share,
    )
    return (
        outs[0][None, None], outs[1][None, None], outs[2][None, None], outs[3][None],
        outs[4][None],
    )


def solution(mesh):
    return jax.shard_map(
        functools.partial(local, mesh.shape["section"], mesh.shape["expert"]),
        mesh=mesh,
        in_specs=(
            P(None, "expert", None),
            P(None, "expert"),
            P("section", None, "expert", None),
            P("section", None, "expert"),
            P("section", "expert", None, None),
            P("section", "expert", None, None),
            P("section", "expert", None, None),
            P("section", None, None),
            P("section", None, None),
            P(),
        ),
        out_specs=(
            P("section", "expert", None, None),
            P("section", "expert", None, None),
            P("section", "expert", None, None),
            P("section", "expert", None),
            P("section", None, "expert"),
        ),
        check_vma=False,
    )
```

```python
import functools

import jax
import jax.numpy as jnp
from jax import lax
from jax.experimental import pallas as pl
from jax.experimental.pallas import tpu as pltpu
from jax.sharding import PartitionSpec as P

epsilon = 1e-06
MESH = pl.DeviceIdType.MESH
f32, bf16 = jnp.float32, jnp.bfloat16
TILE = 16
PIECES = 4
NN = (((1,), (0,)), ((), ()))
NT = (((1,), (1,)), ((), ()))
TN = (((0,), (0,)), ((), ()))


def mm(left, right, dims=NN):
    return lax.dot_general(left, right, dims, preferred_element_type=f32)


def rms_scale(widened):
    return lax.rsqrt(jnp.mean(widened * widened, axis=-1, keepdims=True) + epsilon)


def columns_of(values, piece, at):
    return values[:, at * piece : (at + 1) * piece]


def norm_back(widened, row_scale, grad_norm):
    inner_mean = jnp.mean(grad_norm * widened, axis=-1, keepdims=True)
    return row_scale * grad_norm - widened * (row_scale * row_scale * row_scale) * inner_mean


def sigmoid(values):
    return jax.nn.sigmoid(values)


def kernel(
    sections, experts, slot,
    feat, label, ids, gate_row, gate_w, up_w, down_w, low_in, low_out, head,
    slots, slot_scale, slot_grads, hidden, grad_gate, grad_up, share_in,
    h_in, h_out, g_in, gates, spread, gather, outgoing, back,
    gate_act, gate_slope,
    low, low_all, low_rows, low_grads, low_scale, low_act, low_slope, low_pre, parts, shares,
    x_send, x_recv, hop_send, hop_recv, lw_send, lw_recv, lb_send, lb_recv,
    p_send, p_recv, q_send, q_recv,
):
    micro, rows, width = feat.shape
    count = experts * slot
    piece = width // experts
    part_width = width // PIECES
    last = sections - 1
    sec, me = lax.axis_index("section"), lax.axis_index("expert")
    mine = pl.ds(pl.multiple_of(me * piece, piece), piece)

    barrier = pltpu.get_barrier_semaphore()

    @pl.loop(1, experts)
    def _(k):
        pl.semaphore_signal(
            barrier, inc=1, device_id=(sec, lax.rem(me + k, experts)), device_id_type=MESH
        )

    @pl.loop(1, sections)
    def _(k):
        pl.semaphore_signal(
            barrier, inc=1, device_id=(lax.rem(sec + k, sections), me), device_id_type=MESH
        )

    pl.semaphore_wait(barrier, experts + sections - 2)

    def low_copy(source):
        return pltpu.make_async_remote_copy(
            src_ref=low.at[:, mine, :], dst_ref=low_all.at[source, :, mine, :],
            send_sem=lw_send, recv_sem=lw_recv.at[source],
            device_id=(last, me), device_id_type=MESH,
        )

    def low_spread(peer, owner):
        part = pl.ds(pl.multiple_of(owner * piece, piece), piece)
        view = low_all.at[pl.ds(0, last), :, part, :]
        return pltpu.make_async_remote_copy(
            src_ref=view, dst_ref=view, send_sem=lb_send.at[peer], recv_sem=lb_recv.at[owner],
            device_id=(sec, peer), device_id_type=MESH,
        )

    def exchange(phase, m, c, peer, owner, target):
        return pltpu.make_async_remote_copy(
            src_ref=outgoing.at[m, c, peer], dst_ref=target.at[m, c, owner],
            send_sem=x_send.at[phase, m, c, peer], recv_sem=x_recv.at[phase, m, c, owner],
            device_id=(sec, peer), device_id_type=MESH,
        )

    def send_slots(phase, m, c, target):
        @pl.loop(1, experts)
        def _(k):
            exchange(phase, m, c, lax.rem(me + k, experts), me, target).start()

        target[m, c, me] = outgoing[m, c, me]

    def wait_slots(phase, m, c, target):
        @pl.loop(1, experts)
        def _(k):
            peer = lax.rem(me + k, experts)
            exchange(phase, m, c, peer, peer, target).wait_recv()

    def wait_sent(phase, m, c, target):
        @pl.loop(1, experts)
        def _(k):
            exchange(phase, m, c, lax.rem(me + k, experts), me, target).wait_send()

    def hop(way, m, c, source, target, to):
        return pltpu.make_async_remote_copy(
            src_ref=source.at[m, c], dst_ref=target.at[m, c],
            send_sem=hop_send.at[way, m, c], recv_sem=hop_recv.at[way, m, c],
            device_id=(to, me), device_id_type=MESH,
        )

    below = lax.rem(sec + 1, sections)
    above = lax.rem(sec + sections - 1, sections)

    def eye(size):
        first = lax.broadcasted_iota(jnp.int32, (size, size), 0)
        second = lax.broadcasted_iota(jnp.int32, (size, size), 1)
        return first, second

    def column(values):
        first, second = eye(values.shape[1])
        return jnp.sum(jnp.where(first == second, values, 0.0), axis=1, keepdims=True)

    def prepare_low():
        first, second = eye(low_out.shape[0])
        low[0] = low_in[...]
        low[1] = mm(low_out[...], jnp.where(first == second, 1.0, 0.0).astype(bf16), TN).astype(bf16)

        @pl.when(sec < last)
        def _():
            low_copy(sec).start()

    @pl.when(sec > 0)
    def _():
        prepare_low()

    def prepare_routes(m):
        ids_row = ids[m].astype(f32)
        ids_col = column(ids_row)
        same = jnp.where(ids_col == ids_row, 1.0, 0.0)
        first, second = eye(rows)
        rank_col = jnp.sum(jnp.where(second < first, same, 0.0), axis=1, keepdims=True)
        rank_row = jnp.sum(jnp.where(first < second, same, 0.0), axis=0, keepdims=True)
        grid_row = lax.broadcasted_iota(jnp.int32, (count, rows), 0).astype(f32)
        grid_col = lax.broadcasted_iota(jnp.int32, (rows, count), 1).astype(f32)
        spread[m] = jnp.where(grid_row == ids_row * slot + rank_row, 1.0, 0.0).astype(bf16)
        gather[m] = jnp.where(grid_col == ids_col * slot + rank_col, 1.0, 0.0).astype(bf16)
        gates[m] = column(gate_row[m])

    for m in range(micro):
        prepare_routes(m)

    @pl.when(sec == last)
    def _():
        @pl.loop(0, last)
        def _(source):
            low_copy(source).wait_recv()

        @pl.loop(1, experts)
        def _(k):
            low_spread(lax.rem(me + k, experts), me).start()

        low_all[last] = low[...]

    group = min(experts, 8)
    wide = group * slot

    def in_groups(run):
        if experts == group:
            run(pl.ds(0, group), pl.ds(0, wide))
        else:

            @pl.loop(0, experts // group)
            def _(turn):
                run(
                    pl.ds(pl.multiple_of(turn * group, group), group),
                    pl.ds(pl.multiple_of(turn * wide, wide), wide),
                )

    def place(m, c, values):
        def run(peers, lines):
            placed = mm(spread[m, lines], values).astype(bf16)
            outgoing[m, c, peers] = placed.reshape(group, slot, part_width)

        in_groups(run)

    def cols(c):
        return pl.ds(c * part_width, part_width)

    def lines_of(buffer, m, c, peers):
        return buffer[m, c, peers].reshape(wide, part_width)

    def send_forward(m):
        for c in range(PIECES):
            @pl.when(sec == 0)
            def _():
                h_in[m, c] = feat[m, :, cols(c)]

            @pl.when(sec > 0)
            def _():
                hop(0, m, c, h_out, h_in, below).wait_recv()

            place(m, c, h_in[m, c])
            send_slots(0, m, c, slots)

    def serve_forward(m):
        for c in range(PIECES):
            wait_slots(0, m, c, slots)

        def inward(peers, lines):
            total = 0.0
            for c in range(PIECES):
                values = lines_of(slots, m, c, peers).astype(f32)
                total = total + jnp.sum(values * values, axis=-1, keepdims=True)
            row_scale = lax.rsqrt(total / width + epsilon)
            slot_scale[m, lines] = row_scale
            gate_pre, up_pre = 0.0, 0.0
            for c in range(PIECES):
                values = lines_of(slots, m, c, peers).astype(f32)
                normed = (values * row_scale).astype(bf16)
                gate_pre = gate_pre + mm(normed, gate_w[cols(c), :])
                up_pre = up_pre + mm(normed, up_w[cols(c), :])
            gate_sig = sigmoid(gate_pre)
            act = gate_pre * gate_sig
            gate_act[m, lines] = act
            hidden[m, lines] = (act * up_pre).astype(bf16)
            gate_slope[m, lines] = up_pre * (gate_sig * (1.0 + gate_pre * (1.0 - gate_sig)))

        in_groups(inward)
        for c in range(PIECES):
            wait_sent(0, m, c, slots)

            def outward(peers, lines):
                served = mm(hidden[m, lines], down_w[:, cols(c)]).astype(bf16)
                outgoing[m, c, peers] = served.reshape(group, slot, part_width)

            in_groups(outward)
            send_slots(1, m, c, back)

    def end_forward(m):
        for c in range(PIECES):
            wait_slots(1, m, c, back)
            picked = mm(gather[m], back[m, c].reshape(count, part_width))
            h_out[m, c] = (h_in[m, c].astype(f32) + gates[m] * picked).astype(bf16)

            @pl.when(sec < last)
            def _():
                hop(0, m, c, h_out, h_in, below).start()

        for c in range(PIECES):
            wait_sent(1, m, c, back)

    def low_layers(m):
        for c in range(PIECES):
            low_rows[last, m, :, cols(c)] = h_out[m, c]

        def forward(step, carry):
            layer = last - step
            values = low_rows[layer, m].astype(f32)
            row_scale = rms_scale(values)
            low_scale[layer, m] = row_scale
            inner_pre = mm((values * row_scale).astype(bf16), low_all[layer, 0])
            inner_sig = sigmoid(inner_pre)
            inner_act = (inner_pre * inner_sig).astype(bf16)
            low_act[layer, m] = inner_act
            low_slope[layer, m] = inner_sig * (1.0 + inner_pre * (1.0 - inner_sig))
            result = (values + mm(inner_act, low_all[layer, 1], NT)).astype(bf16)

            @pl.when(layer > 0)
            def _():
                low_rows[layer - 1, m] = result

            @pl.when(layer == 0)
            def _():
                low_grads[0, m] = result

            return carry

        lax.fori_loop(0, sections, forward, 0)
        values = low_grads[0, m].astype(f32)
        row_scale = rms_scale(values)
        logits = row_scale * jnp.sum(values * head[...], axis=1, keepdims=True)
        grad_logit = sigmoid(logits) - column(label[m].astype(f32))
        low_grads[0, m] = norm_back(values, row_scale, grad_logit * head[...]).astype(bf16)

        def backward(layer, carry):
            values = low_rows[layer, m].astype(f32)
            row_scale = low_scale[layer, m]
            grads = low_grads[layer, m]
            grad_pre = (mm(grads, low_all[layer, 1]) * low_slope[layer, m]).astype(bf16)
            low_pre[layer, m] = grad_pre
            grad_norm = mm(grad_pre, low_all[layer, 0], NT)
            result = (grads.astype(f32) + norm_back(values, row_scale, grad_norm)).astype(bf16)

            @pl.when(layer < last)
            def _():
                low_grads[layer + 1, m] = result

            @pl.when(layer == last)
            def _():
                for c in range(PIECES):
                    g_in[m, c] = columns_of(result, part_width, c)

            return carry

        lax.fori_loop(0, sections, backward, 0)

    def send_backward(m):
        for c in range(PIECES):
            @pl.when(sec < last)
            def _():
                hop(1, m, c, h_out, g_in, above).wait_recv()

            place(m, c, (gates[m] * g_in[m, c].astype(f32)).astype(bf16))
            send_slots(2, m, c, slot_grads)

    def serve_backward(m):
        for c in range(PIECES):
            wait_slots(2, m, c, slot_grads)

        def slope(peers, lines):
            grad_hidden = 0.0
            for c in range(PIECES):
                grads = lines_of(slot_grads, m, c, peers)
                grad_hidden = grad_hidden + mm(grads, down_w[:, cols(c)], NT)
            grad_gate[m, lines] = (grad_hidden * gate_slope[m, lines]).astype(bf16)
            grad_up[m, lines] = (grad_hidden * gate_act[m, lines]).astype(bf16)

        in_groups(slope)
        for c in range(PIECES):
            wait_sent(2, m, c, slot_grads)

        @pl.when(sec > 0)
        def _():
            def answer(peers, lines):
                row_scale = slot_scale[m, lines]
                products, total = [], 0.0
                for c in range(PIECES):
                    grads = mm(grad_gate[m, lines], gate_w[cols(c), :], NT) + mm(
                        grad_up[m, lines], up_w[cols(c), :], NT
                    )
                    values = lines_of(slots, m, c, peers).astype(f32)
                    total = total + jnp.sum(grads * values, axis=-1, keepdims=True)
                    products.append(grads)
                weight = row_scale * row_scale * row_scale * (total / width)
                for c in range(PIECES):
                    values = lines_of(slots, m, c, peers).astype(f32)
                    result = (row_scale * products[c] - values * weight).astype(bf16)
                    outgoing[m, c, peers] = result.reshape(group, slot, part_width)
                    if experts == group:
                        send_slots(3, m, c, back)

            in_groups(answer)
            if experts > group:
                for c in range(PIECES):
                    send_slots(3, m, c, back)

    def end_backward(m):
        @pl.when(sec > 0)
        def _():
            for c in range(PIECES):
                wait_slots(3, m, c, back)
                picked = mm(gather[m], back[m, c].reshape(count, part_width))

                @pl.when(sec < last)
                def _():
                    hop(0, m, c, h_out, h_in, below).wait_send()

                h_out[m, c] = (g_in[m, c].astype(f32) + picked).astype(bf16)
                hop(1, m, c, h_out, g_in, above).start()

            for c in range(PIECES):
                wait_sent(3, m, c, back)

        @pl.when(sec == 0)
        def _():
            for c in range(PIECES):
                hop(0, m, c, h_out, h_in, below).wait_send()

    send_forward(0)

    @pl.when(sec == 0)
    def _():
        prepare_low()

    for m in range(micro):
        if m:
            send_forward(m)

            @pl.when(sec == last)
            def _():
                if m == 1:
                    @pl.loop(1, experts)
                    def _(k):
                        peer = lax.rem(me + k, experts)
                        low_spread(peer, peer).wait_recv()

                low_layers(m - 1)
                send_backward(m - 1)

        serve_forward(m)
        if m:
            @pl.when(sec == last)
            def _():
                serve_backward(m - 1)

        end_forward(m)
        if m > 1:
            @pl.when(sec == last)
            def _():
                end_backward(m - 2)

    final = micro - 1

    @pl.when(sec == last)
    def _():
        if micro == 1:
            @pl.loop(1, experts)
            def _(k):
                peer = lax.rem(me + k, experts)
                low_spread(peer, peer).wait_recv()

        low_layers(final)
        send_backward(final)
        if micro > 1:
            end_backward(final - 1)
        serve_backward(final)
        end_backward(final)

    @pl.when(sec < last)
    def _():
        for m in range(micro):
            send_backward(m)
            serve_backward(m)
            end_backward(m)

    half = experts // 2
    side, chip = lax.rem(me, 2), me // 2
    sibling = me + 1 - 2 * side

    def part_of(owner):
        return pl.ds(pl.multiple_of(owner * piece, piece), piece)

    def pair_copy(j, parity):
        return pltpu.make_async_remote_copy(
            src_ref=low_all.at[:, :, part_of(2 * j + parity), :], dst_ref=parts.at[j],
            send_sem=p_send.at[j], recv_sem=p_recv.at[j],
            device_id=(sec, sibling), device_id_type=MESH,
        )

    def share_copy(to, origin):
        return pltpu.make_async_remote_copy(
            src_ref=low_all.at[:, :, part_of(2 * to + side), :], dst_ref=parts.at[half + origin],
            send_sem=p_send.at[half + to], recv_sem=p_recv.at[half + origin],
            device_id=(sec, 2 * to + side), device_id_type=MESH,
        )

    def share_out(section):
        return pltpu.make_async_remote_copy(
            src_ref=shares.at[section], dst_ref=share_in, send_sem=q_send.at[section],
            recv_sem=q_recv, device_id=(section, me), device_id_type=MESH,
        )

    @pl.when(sec == last)
    def _():
        @pl.loop(1, experts)
        def _(k):
            low_spread(lax.rem(me + k, experts), me).wait_send()

        def products(layer, carry):
            normed = (low_rows[layer].astype(f32) * low_scale[layer]).astype(bf16)
            normed = normed.reshape(micro * rows, width)
            grads = low_grads[layer].reshape(micro * rows, width)
            pre = low_pre[layer].reshape(micro * rows, -1)
            act = low_act[layer].reshape(micro * rows, -1)
            low_all[layer, 0] = mm(normed, pre, TN).astype(bf16)
            low_all[layer, 1] = mm(grads, act, TN).astype(bf16)
            return carry

        lax.fori_loop(0, sections, products, 0)

        @pl.loop(1, half + 1)
        def _(k):
            pair_copy(lax.rem(chip + k, half), 1 - side).start()

        @pl.loop(1, half + 1)
        def _(k):
            to = lax.rem(chip + k, half)
            pair_copy(to, side).wait_recv()

            def join(layer, carry):
                own = low_all[layer, :, part_of(2 * to + side), :].astype(f32)
                joined = own + parts[to, layer].astype(f32)
                low_all[layer, :, part_of(2 * to + side), :] = joined.astype(bf16)
                return carry

            lax.fori_loop(0, sections, join, 0)

            @pl.when(k < half)
            def _():
                share_copy(to, chip).start()

        @pl.loop(1, half)
        def _(k):
            origin = lax.rem(chip + k, half)
            share_copy(origin, origin).wait_recv()

        def total(layer, carry):
            def add(k, acc):
                return acc + parts[half + lax.rem(chip + k, half), layer].astype(f32)

            acc = lax.fori_loop(1, half, add, low_all[layer, :, mine, :].astype(f32))
            shares[layer] = acc.astype(bf16)
            return carry

        lax.fori_loop(0, sections, total, 0)

        @pl.loop(0, last)
        def _(section):
            share_out(section).start()

        share_in[...] = shares[last]

        @pl.loop(0, last)
        def _(section):
            share_out(section).wait_send()

        @pl.loop(1, half)
        def _(k):
            share_copy(lax.rem(chip + k, half), chip).wait_send()

        @pl.loop(0, half)
        def _(j):
            pair_copy(j, 1 - side).wait_send()

    @pl.when(sec < last)
    def _():
        low_copy(sec).wait_send()
        share_out(last).wait_recv()

    @pl.when(sec > 0)
    def _():
        for m in range(micro):
            for c in range(PIECES):
                hop(1, m, c, h_out, g_in, above).wait_send()


def products_kernel(
    slots, scale, slot_grads, hidden, grad_gate, grad_up, share,
    out_gate, out_up, out_down, out_in, out_out,
):
    flat = hidden.shape[0]
    values = slots[...].reshape(flat, -1).astype(f32)
    normed = (values * scale[...].reshape(flat, 1)).astype(bf16)
    out_gate[...] = mm(normed, grad_gate[...], TN)
    out_up[...] = mm(normed, grad_up[...], TN)
    out_down[...] = mm(hidden[...], slot_grads[...].reshape(flat, -1), TN)

    @pl.when(pl.program_id(0) == 0)
    def _():
        out_in[...] = share[0].astype(f32)
        size = share.shape[2]
        first = lax.broadcasted_iota(jnp.int32, (size, size), 0)
        second = lax.broadcasted_iota(jnp.int32, (size, size), 1)
        unit = jnp.where(first == second, 1.0, 0.0).astype(bf16)
        out_out[...] = mm(unit, share[1], NT)


def local(
    sections, experts,
    features, labels, routes, route_gates, gate_weight, up_weight, down_weight,
    lowrank_in, lowrank_out, head_weight,
):
    micro, rows, width = features.shape
    inner_width, rank = gate_weight.shape[-1], lowrank_in.shape[-1]
    capacity = min(rows, max(2, 3 * rows // (2 * experts)))
    slot = -(-capacity // TILE) * TILE
    count, piece = experts * slot, width // experts
    flat = micro * count
    vmem = pl.BlockSpec(memory_space=pltpu.VMEM)
    dma = pltpu.SemaphoreType.DMA
    step = width // PIECES
    buffer = pltpu.VMEM((micro, PIECES, experts, slot, step), bf16)
    row_buffer = pltpu.VMEM((micro, PIECES, rows, step), bf16)
    slot_shape = jax.ShapeDtypeStruct((micro, PIECES, experts, slot, step), bf16)
    inner_shape = jax.ShapeDtypeStruct((micro, count, inner_width), bf16)
    inner = pltpu.VMEM((micro, count, inner_width), f32)
    low_buffer = pltpu.VMEM((sections, micro, rows, width), bf16)
    made = pl.pallas_call(
        functools.partial(kernel, sections, experts, slot),
        out_shape=(
            slot_shape, jax.ShapeDtypeStruct((micro, count, 1), f32), slot_shape, inner_shape, inner_shape, inner_shape,
            jax.ShapeDtypeStruct((2, piece, rank), bf16),
        ),
        in_specs=[vmem] * 10,
        out_specs=(vmem,) * 7,
        scratch_shapes=[
            row_buffer, row_buffer, row_buffer,
            pltpu.VMEM((micro, rows, 1), f32),
            pltpu.VMEM((micro, count, rows), bf16),
            pltpu.VMEM((micro, rows, count), bf16),
            buffer, buffer, inner, inner,
            pltpu.VMEM((2, width, rank), bf16),
            pltpu.VMEM((sections, 2, width, rank), bf16),
            low_buffer, low_buffer,
            pltpu.VMEM((sections, micro, rows, 1), f32),
            pltpu.VMEM((sections, micro, rows, rank), bf16),
            pltpu.VMEM((sections, micro, rows, rank), f32),
            pltpu.VMEM((sections, micro, rows, rank), bf16),
            pltpu.VMEM((experts, sections, 2, piece, rank), bf16),
            pltpu.VMEM((sections, 2, piece, rank), bf16),
            dma((4, micro, PIECES, experts)), dma((4, micro, PIECES, experts)),
            dma((2, micro, PIECES)), dma((2, micro, PIECES)),
            dma, dma((sections,)),
            dma((experts,)), dma((experts,)),
            dma((experts,)), dma((experts,)),
            dma((sections,)), dma,
        ],
        compiler_params=pltpu.CompilerParams(
            collective_id=0, has_side_effects=True, vmem_limit_bytes=60 * 1024 * 1024
        ),
    )(
        features, labels.reshape(micro, 1, rows), routes.reshape(micro, 1, rows),
        route_gates.reshape(micro, 1, rows), gate_weight[0, 0], up_weight[0, 0],
        down_weight[0, 0], lowrank_in[0], lowrank_out[0], head_weight[None, :],
    )
    slots, scale, slot_grads, hidden, grad_gate, grad_up, share = made
    wide = pl.BlockSpec((micro, 1, count, step), lambda i: (0, i, 0, 0))
    narrow = pl.BlockSpec((flat, inner_width), lambda i: (0, 0))
    tall = pl.BlockSpec((step, inner_width), lambda i: (i, 0))
    outs = pl.pallas_call(
        products_kernel,
        grid=(PIECES,),
        out_shape=(
            jax.ShapeDtypeStruct((width, inner_width), f32),
            jax.ShapeDtypeStruct((width, inner_width), f32),
            jax.ShapeDtypeStruct((inner_width, width), f32),
            jax.ShapeDtypeStruct((piece, rank), f32),
            jax.ShapeDtypeStruct((rank, piece), f32),
        ),
        in_specs=[
            wide, pl.BlockSpec((micro, count, 1), lambda i: (0, 0, 0)), wide, narrow, narrow, narrow,
            pl.BlockSpec((2, piece, rank), lambda i: (0, 0, 0)),
        ],
        out_specs=(
            tall, tall, pl.BlockSpec((inner_width, step), lambda i: (0, i)),
            pl.BlockSpec((piece, rank), lambda i: (0, 0)),
            pl.BlockSpec((rank, piece), lambda i: (0, 0)),
        ),
        compiler_params=pltpu.CompilerParams(vmem_limit_bytes=60 * 1024 * 1024),
    )(
        slots.reshape(micro, PIECES, count, step), scale,
        slot_grads.reshape(micro, PIECES, count, step),
        hidden.reshape(flat, inner_width), grad_gate.reshape(flat, inner_width),
        grad_up.reshape(flat, inner_width), share,
    )
    return (
        outs[0][None, None], outs[1][None, None], outs[2][None, None], outs[3][None],
        outs[4][None],
    )


def solution(mesh):
    return jax.shard_map(
        functools.partial(local, mesh.shape["section"], mesh.shape["expert"]),
        mesh=mesh,
        in_specs=(
            P(None, "expert", None),
            P(None, "expert"),
            P("section", None, "expert", None),
            P("section", None, "expert"),
            P("section", "expert", None, None),
            P("section", "expert", None, None),
            P("section", "expert", None, None),
            P("section", None, None),
            P("section", None, None),
            P(),
        ),
        out_specs=(
            P("section", "expert", None, None),
            P("section", "expert", None, None),
            P("section", "expert", None, None),
            P("section", "expert", None),
            P("section", None, "expert"),
        ),
        check_vma=False,
    )
```
